256 devices in a mesh: slab: 64 (over y, x_hi, z), mode: 4 (over x_lo, core).
Axes of the slice: x: 4 (x_hi: 2, x_lo: 2; x = x_hi * 2 + x_lo), y: 4, z: 8, core: 2. Of those that a mesh axis runs over, the one named last changes fastest.
Arguments:
- eigvec: bfloat16 [81920, 3, 1024], P('slab', None, 'mode'), may hold values from -6 to 6
- species: int32 [81920], P('slab'), may hold values from 0 to 3
- mode_cot: float32 [1024], P('mode'), may hold values from -4 to 4
- neighbours: int32 [81920, 16], P('slab'), may hold values from 0 to 2560, as said below
- pair_features: bfloat16 [1310720, 128], P(('slab', 'mode')), may hold values from -130 to 130
- w_in: bfloat16 [128, 256], replicated, may hold values from -0.5 to 0.5
- b_in: float32 [256], replicated, may hold values from -3 to 3
- w_out: bfloat16 [9, 256], replicated, may hold values from -0.375 to 0.375
Outputs:
- features_grad: bfloat16 [1310720, 128], P(('slab', 'mode'))
- grad_w_in: float32 [128, 256], replicated
- grad_b_in: float32 [256], replicated
- grad_w_out: float32 [9, 256], replicated
The draws below stay inside these ranges and needn't reach their ends.
Inputs may be any that keep to these rules, and one draw needn't show every extreme that they name: `neighbours`: atom r of a slab (0 to 1279) lists extended indices from r to r + 1280; extended index x stands for atom (slab * 1280 + x - 640) mod 81920; the value 1280 + 2 * 640 marks an empty slot.
All inputs are finite; a program needn't handle non-finite values.
Results may differ from the reference program's by a relative error of at most 0.019.
Values may be sent and summed in bfloat16 or wider, within the bound.
No kernel may reach another device: no remote copies, remote signals or barrier semaphores. Data moves between devices by JAX's collectives and lax.ppermute only.
A program may use at most 64 MiB of HBM per device.

```python
import math
import jax
import jax.numpy as jnp
from jax import lax

A_DEV = 1280
RIM = 640
NBR = 16
MODES = 1024
F = 128
H = 256
ATOMS = 81920
PAIRS = 1310720
N_SLAB = 64


def draw_neighbours(key, part):
    first_key, second_key = jax.random.split(key)
    local = jnp.arange(ATOMS, dtype=jnp.int32) % A_DEV
    slot = jnp.arange(NBR, dtype=jnp.int32)
    offset = jax.random.randint(first_key, (ATOMS, NBR), 0, 2 * RIM + 1)
    offset = jnp.where((local[:, None] == 0) & (slot[None, :] == 0), 0, offset)
    counts = jax.random.randint(second_key, (ATOMS,), 10, NBR + 1)
    counts = jnp.where(local == 0, 10, counts)
    live_slot = slot[None, :] < counts[:, None]
    return jnp.where(live_slot, local[:, None] + offset, A_DEV + 2 * RIM).astype(jnp.int32)


def draw_pair_features(key, part):
    col_key, base_key = jax.random.split(key, 2)
    column_scale = jnp.exp(jax.random.uniform(col_key, (F,), minval=0.0, maxval=math.log(10.0)))
    ramp = 1.0 + 2.0 * jnp.arange(PAIRS, dtype=jnp.float32) / PAIRS
    base = jnp.clip(jax.random.normal(base_key, (PAIRS, F)), -4.0, 4.0)
    return (base * ramp[:, None] * column_scale[None, :]).astype(jnp.bfloat16)


def with_ends(drawn, rng, low, high):
    longest = drawn.shape.index(max(drawn.shape))
    spots = []
    for shift in (0, 1):
        where = [jax.random.randint(jax.random.fold_in(rng, axis), (), 0, length) for axis, length in enumerate(drawn.shape)]
        where[longest] = (where[longest] + shift) % drawn.shape[longest]
        spots.append(tuple(where))
    return drawn.at[spots[0]].set(low).at[spots[1]].set(high)


def block_scale(own_key, shape, shards, low, high):
    gain = 1.0
    for position, parts in shards:
        heights = jax.random.uniform(jax.random.fold_in(jax.random.fold_in(own_key, 6), position), (parts,), jnp.float32, low / len(shards), high / len(shards))
        gain = gain * jnp.repeat(jnp.exp(heights), shape[position] // parts).reshape((-1,) + (1,) * (len(shape) - 1 - position))
    return gain


def centred(rng, dims, width, limit, shards=(), kind=jnp.bfloat16):
    values = width * jax.random.normal(rng, dims, jnp.float32)
    if shards:
        values = values * block_scale(rng, dims, shards, -0.22, 0.18)
    return jnp.clip(values, -limit, limit).astype(kind)


def setup_inputs(seed: int = 0) -> dict:
    keys = jax.random.split(jax.random.key(seed), 9)
    return {
        "eigvec": centred(keys[0], (ATOMS, 3, MODES), 1.0, 6.0, ((0, 64), (2, 4))),
        "species": with_ends(jax.random.randint(keys[1], (ATOMS,), 0, 4), jax.random.fold_in(keys[1], 1), 0, 3).astype(jnp.int32),
        "mode_cot": centred(keys[2], (MODES,), 1.0, 4.0, ((0, 4),), jnp.float32),
        "neighbours": draw_neighbours(jax.random.fold_in(keys[8], 71), 0),
        "pair_features": draw_pair_features(jax.random.fold_in(keys[8], 71), 0),
        "w_in": centred(keys[5], (F, H), F ** -0.5, 0.5),
        "b_in": centred(keys[6], (H,), 0.5, 3.0, (), jnp.float32),
        "w_out": centred(keys[7], (9, H), H ** -0.5, 0.375),
    }


MASS_TABLE = (1.35, 2.94, 2.79, 2.95)
CLIP_NORM = 100.0

def atom_masses(species):
    kinds = jnp.arange(4, dtype=jnp.int32)
    onehot = (species[:, None] == kinds[None, :]).astype(jnp.float32)
    return lax.optimization_barrier(jnp.sum(onehot * jnp.asarray(MASS_TABLE, jnp.float32)[None, :], axis=1))

def mlp_backward(features, pair_cot, w_in, b_in, w_out):
    preact = jnp.dot(features, w_in, preferred_element_type=jnp.float32) + b_in[None, :]
    sigmoid_pre = jax.nn.sigmoid(preact)
    hidden = (preact * sigmoid_pre).astype(jnp.bfloat16)
    hidden_cot = lax.dot_general(pair_cot, w_out, (((0,), (0,)), ((), ())), preferred_element_type=jnp.float32)
    pre_cot = (hidden_cot * sigmoid_pre * (1.0 + preact * (1.0 - sigmoid_pre))).astype(jnp.bfloat16)
    features_grad = lax.dot_general(pre_cot, w_in, (((1,), (1,)), ((), ())), preferred_element_type=jnp.float32).astype(jnp.bfloat16)
    grad_w_in = lax.dot_general(features, pre_cot, (((0,), (0,)), ((), ())), preferred_element_type=jnp.float32)
    grad_b_in = lax.optimization_barrier(jnp.sum(pre_cot.astype(jnp.float32), axis=0))
    grad_w_out = jnp.dot(pair_cot, hidden, preferred_element_type=jnp.float32)
    return (features_grad, grad_w_in, grad_b_in, grad_w_out)

def reference(eigvec, species, mode_cot, neighbours, pair_features, w_in, b_in, w_out):
    inv_root = lax.rsqrt(atom_masses(species))
    scaled = (eigvec.astype(jnp.float32) * inv_root[:, None, None]).astype(jnp.bfloat16)
    weighted = (scaled.astype(jnp.float32) * mode_cot[None, None, :]).astype(jnp.bfloat16)
    sentinel = A_DEV + 2 * RIM

    def per_slab(carry, slab_index):
        first_row = slab_index * A_DEV
        weighted_rows = lax.dynamic_slice_in_dim(weighted, first_row, A_DEV, 0).astype(jnp.float32)
        own_rows = lax.dynamic_slice_in_dim(scaled, first_row, A_DEV, 0).astype(jnp.float32)
        nbr_rows = lax.dynamic_slice_in_dim(neighbours, first_row, A_DEV, 0)
        live_mask = nbr_rows < sentinel
        partner_index = jnp.where(live_mask, (first_row + nbr_rows - RIM) % ATOMS, 0).astype(jnp.int32)
        partners = jnp.take(scaled, partner_index.reshape(-1), axis=0).reshape(A_DEV, NBR, 3, MODES).astype(jnp.float32)
        pair_terms = jnp.einsum('iam,ikbm->abik', weighted_rows, partners, precision=lax.Precision.HIGHEST).reshape(9, A_DEV, NBR)
        self_terms = jnp.einsum('iam,ibm->abi', weighted_rows, own_rows, precision=lax.Precision.HIGHEST).reshape(9, A_DEV)
        pair_cot = ((pair_terms - self_terms[:, :, None]) * live_mask[None].astype(jnp.float32)).astype(jnp.bfloat16)
        pair_cot = pair_cot.reshape(9, A_DEV * NBR)
        features = lax.dynamic_slice_in_dim(pair_features, first_row * NBR, A_DEV * NBR, 0)
        features_grad, part_w_in, part_b_in, part_w_out = mlp_backward(features, pair_cot, w_in, b_in, w_out)
        return ((carry[0] + part_w_in, carry[1] + part_b_in, carry[2] + part_w_out), features_grad)
    start = (jnp.zeros((F, H), jnp.float32), jnp.zeros((H,), jnp.float32), jnp.zeros((9, H), jnp.float32))
    sums, grads = lax.scan(per_slab, start, jnp.arange(N_SLAB, dtype=jnp.int32))
    raw_w_in, raw_b_in, raw_w_out = sums
    norm_sq = jnp.sum(raw_w_in * raw_w_in) + jnp.sum(raw_b_in * raw_b_in) + jnp.sum(raw_w_out * raw_w_out)
    factor = jnp.minimum(1.0, CLIP_NORM / jnp.sqrt(norm_sq + 1e-06))
    return (grads.reshape(PAIRS, F), raw_w_in * factor, raw_b_in * factor, raw_w_out * factor)
```

```python
import functools

import jax
import jax.numpy as jnp
from jax import lax
from jax.experimental import pallas as pl
from jax.experimental.pallas import tpu as pltpu
from jax.sharding import PartitionSpec as P

MASS_TABLE = (1.35, 2.94, 2.79, 2.95)
CLIP_NORM = 100.0
T = 128
ATOMS = 1280
RIM = 640
BLOCKS = ATOMS // T
REACH = RIM // T
GROUPS = ATOMS // 8
QUARTER = GROUPS // 4
F32, BF16 = jnp.float32, jnp.bfloat16
VMEM = pl.BlockSpec(memory_space=pltpu.VMEM)
SMEM = pl.BlockSpec(memory_space=pltpu.SMEM)
PARAMS = pltpu.CompilerParams(vmem_limit_bytes=40 << 20)


def nt_dot(x, y):
    return lax.dot_general(x, y, (((1,), (1,)), ((), ())), preferred_element_type=F32)


def tn_dot(x, y):
    return lax.dot_general(x, y, (((0,), (0,)), ((), ())), preferred_element_type=F32)


def scale_kernel(eig, species, high, low):
    def half(base, out):
        for blk in range(REACH):
            rows = slice(base + blk * T, base + (blk + 1) * T)
            kind = species[:, rows]
            mass = jnp.full(kind.shape, MASS_TABLE[3], F32)
            for k in range(3):
                mass = jnp.where(kind == k, MASS_TABLE[k], mass)
            inv = jnp.broadcast_to(lax.rsqrt(mass), (T, T)).T
            inv = jnp.concatenate([inv, inv], axis=1)
            for a in range(3):
                out[a, blk * T:(blk + 1) * T, :] = (eig[a, rows, :].astype(F32) * inv).astype(BF16)

    half(RIM, high)
    half(0, low)


def add_tile(left, right, tile, lane, where_tile, acc):
    dense = nt_dot(left, right)
    here = where_tile == tile
    for a in range(3):
        for b in range(3):
            part = dense[a * T:(a + 1) * T, b * T:(b + 1) * T]
            got = jnp.take_along_axis(part, lane, axis=1, mode="promise_in_bounds")
            acc[3 * a + b] = jnp.where(here, got, acc[3 * a + b])


def fold_matrix():
    row = lax.broadcasted_iota(jnp.int32, (T // 8, T), 0)
    col = lax.broadcasted_iota(jnp.int32, (T // 8, T), 1)
    return (col // 8 == row).astype(BF16)


def own_kernel(high, low, mode_cot, nbr_t, out, weighted, lane_ref, tile_ref, stack, acc):
    row = lax.broadcasted_iota(jnp.int32, (T, T), 0)
    col = lax.broadcasted_iota(jnp.int32, (T, T), 1)
    diagonal = (row % 8) == (col // 16)
    cot = mode_cot[...]
    for blk in range(BLOCKS):
        n = nbr_t[:, blk * T:(blk + 1) * T].astype(F32)
        n = jnp.concatenate([n] * 8, axis=0).T.astype(jnp.int32)
        live = diagonal & (n < ATOMS + 2 * RIM)
        tile_ref[blk] = jnp.where(live, n >> 7, -1)
        lane_ref[blk] = n & (T - 1)
        src, base = (low, blk * T) if blk < REACH else (high, blk * T - RIM)
        for a in range(3):
            s = src[a, base:base + T, :]
            stack[blk, a * T:(a + 1) * T, :] = s
            weighted[blk, a * T:(a + 1) * T, :] = (s.astype(F32) * cot).astype(BF16)
    fold = fold_matrix()

    def block(i, carry):
        left = weighted[i]
        lane, where_tile = lane_ref[i], tile_ref[i]
        acc[...] = jnp.zeros_like(acc)

        def tile(j, carry):
            add_tile(left, stack[j], j + REACH, lane, where_tile, acc)
            return carry

        lax.fori_loop(jnp.maximum(i - REACH, 0), jnp.minimum(i + REACH, BLOCKS - 1) + 1, tile, 0)
        mine = stack[i]
        live = where_tile >= 0
        for a in range(3):
            for b in range(3):
                both = left[a * T:(a + 1) * T].astype(F32) * mine[b * T:(b + 1) * T].astype(F32)
                self_term = jnp.sum(both, axis=1, keepdims=True)
                term = jnp.where(live, acc[3 * a + b] - self_term, 0.0)
                folded = jnp.dot(fold, term.astype(BF16), preferred_element_type=F32)
                out[3 * a + b, pl.ds(pl.multiple_of(i * 16, 16), 16), :] = folded
        return carry

    lax.fori_loop(0, BLOCKS, block, 0)


def halo_kernel(mode_index, below, above, weighted, lane_ref, tile_ref, own,
                out0, out1, out2, out3, acc, total):
    fold = fold_matrix()

    def block(src, shift, lo, hi, i):
        left = weighted[i]
        lane, where_tile = lane_ref[i], tile_ref[i]
        acc[...] = jnp.zeros_like(acc)

        def tile(t, carry):
            rows = pl.ds(pl.multiple_of((t - shift) * T, T), T)
            right = jnp.concatenate([src[b, rows, :] for b in range(3)], axis=0)
            add_tile(left, right, t, lane, where_tile, acc)
            return carry

        lax.fori_loop(lo, hi, tile, 0)
        at = pl.ds(pl.multiple_of(i * 16, 16), 16)
        for c in range(9):
            folded = jnp.dot(fold, acc[c].astype(BF16), preferred_element_type=F32)
            total[c, at, :] = own[c, at, :] + folded

    def low_block(i, carry):
        block(below, 0, i, REACH, i)
        return carry

    def high_block(i, carry):
        block(above, 3 * REACH, 3 * REACH, i + 2 * REACH + 1, i)
        return carry

    lax.fori_loop(0, REACH, low_block, 0)
    lax.fori_loop(REACH, BLOCKS, high_block, 0)
    m = mode_index[0]
    for k, out in enumerate((out0, out1, out2, out3)):
        q = lax.rem(m + k, 4)
        out[...] = total[:, pl.ds(pl.multiple_of(q * QUARTER, 8), QUARTER), :].astype(BF16)


CHUNK = 512


def forward_kernel(features, w_in, b_in, hidden, slope):
    pre = jnp.dot(features[...], w_in[...], preferred_element_type=F32) + b_in[...]
    sig = 1.0 / (1.0 + jnp.exp(-pre))
    hidden[...] = (pre * sig).astype(BF16)
    slope[...] = (sig * (1.0 + pre * (1.0 - sig))).astype(BF16)


def backward_kernel(mode_index, p0, p1, p2, p3, features, hidden, slope, w_in, w_out,
                    grad, g0, g1, g2, g3, cot, sums):
    step = pl.program_id(0)

    @pl.when(step == 0)
    def _():
        whole = sum(p[...].astype(F32) for p in (p0, p1, p2, p3))
        whole = jnp.concatenate([whole, jnp.zeros((7, QUARTER, T), F32)], axis=0)
        cot[...] = jnp.swapaxes(whole, 0, 1).astype(BF16)
        sums[...] = jnp.zeros_like(sums)

    per = CHUNK // T
    pair_cot = jnp.concatenate([cot[step * per + g] for g in range(per)], axis=1)
    pre_cot32 = tn_dot(pair_cot, w_out[...]) * slope[...].astype(F32)
    pre_cot = pre_cot32.astype(BF16)
    grad[...] = nt_dot(pre_cot, w_in[...]).astype(BF16)
    part_in = tn_dot(features[...], pre_cot)
    part_out = jnp.dot(pair_cot, hidden[...], preferred_element_type=F32)
    part_b = jnp.sum(pre_cot.astype(F32), axis=0, keepdims=True)
    part_b = jnp.concatenate([part_b, jnp.zeros((7, 256), F32)], axis=0)
    for h in range(2):
        cols = slice(h * T, (h + 1) * T)
        sums[h * 152:h * 152 + 128, :] += part_in[:, cols]
        sums[h * 152 + 128:h * 152 + 144, :] += part_out[:, cols]
        sums[h * 152 + 144:h * 152 + 152, :] += part_b[:, cols]

    @pl.when(step == pl.num_programs(0) - 1)
    def _():
        m = mode_index[0]
        for k, out in enumerate((g0, g1, g2, g3)):
            q = lax.rem(m + k, 4)
            out[...] = sums[pl.ds(pl.multiple_of(q * ROWS, 8), ROWS), :]


SUM_ROWS = 320
ROWS = SUM_ROWS // 4


def finish_kernel(mode_index, c0, c1, c2, c3, grad_w_in, grad_b_in, grad_w_out, whole):
    m = mode_index[0]
    for k, part in enumerate((c0, c1, c2, c3)):
        q = lax.rem(m + 4 - k, 4)
        whole[pl.ds(pl.multiple_of(q * ROWS, 8), ROWS), :] = part[...]
    both = []
    for start, rows in ((0, 128), (128, 9), (144, 1)):
        both.append(jnp.concatenate([whole[h * 152 + start:h * 152 + start + rows, :] for h in range(2)], axis=1))
    w, o, b = both
    norm_sq = jnp.sum(w * w) + jnp.sum(b * b) + jnp.sum(o * o)
    factor = jnp.minimum(1.0, CLIP_NORM / jnp.sqrt(jnp.broadcast_to(norm_sq + 1e-06, (1, 256))))
    grad_w_in[...] = w * factor
    grad_b_in[...] = b * factor
    grad_w_out[...] = o * factor


def shape(dims, dtype=F32):
    return jax.ShapeDtypeStruct(dims, dtype)


def cost(flops, moved):
    return pl.CostEstimate(flops=flops, bytes_accessed=moved, transcendentals=0)


def ring(axis, k):
    n = lax.axis_size(axis)
    return [(i, (i + k) % n) for i in range(n)]


def shards(eigvec, species, mode_cot, neighbours, pair_features, w_in, b_in, w_out):
    eig = jnp.transpose(eigvec, (1, 0, 2))
    m = lax.axis_index("mode").astype(jnp.int32).reshape(1)
    high, low = pl.pallas_call(
        scale_kernel, out_shape=[shape((3, RIM, 256), BF16)] * 2,
        in_specs=[VMEM] * 2, out_specs=[VMEM] * 2, compiler_params=PARAMS,
        cost_estimate=cost(1 << 20, 4 << 20), name="scale",
    )(eig, species.reshape(1, ATOMS))
    below = lax.ppermute(high, "slab", ring("slab", 1))
    above = lax.ppermute(low, "slab", ring("slab", lax.axis_size("slab") - 1))
    own, weighted, lane, tile = pl.pallas_call(
        own_kernel,
        out_shape=[shape((9, GROUPS, T)), shape((BLOCKS, 3 * T, 256), BF16),
                   shape((BLOCKS, T, T), jnp.int32), shape((BLOCKS, T, T), jnp.int32)],
        in_specs=[VMEM] * 4, out_specs=[VMEM] * 4,
        scratch_shapes=[pltpu.VMEM((BLOCKS, 3 * T, 256), BF16), pltpu.VMEM((9, T, T), F32)],
        compiler_params=PARAMS, cost_estimate=cost(12_000_000_000, 6 << 20), name="own",
    )(high, low, mode_cot.reshape(1, 256), neighbours.T)
    slots = pair_features.shape[0]
    steps = slots // CHUNK
    rows_spec = lambda width: pl.BlockSpec((CHUNK, width), lambda s: (s, 0))
    full = lambda *dims: pl.BlockSpec(dims, lambda s: (0,) * len(dims))
    hidden, slope = pl.pallas_call(
        forward_kernel, out_shape=[shape((slots, 256), BF16)] * 2, grid=(steps,),
        in_specs=[rows_spec(128), full(128, 256), full(1, 256)], out_specs=[rows_spec(256)] * 2,
        compiler_params=PARAMS, cost_estimate=cost(4_000_000_000, 7 << 20), name="forward",
    )(pair_features, w_in, b_in.reshape(1, 256))
    parts = pl.pallas_call(
        halo_kernel, out_shape=[shape((9, QUARTER, T), BF16)] * 4,
        in_specs=[SMEM] + [VMEM] * 6, out_specs=[VMEM] * 4,
        scratch_shapes=[pltpu.VMEM((9, T, T), F32), pltpu.VMEM((9, GROUPS, T), F32)],
        compiler_params=PARAMS, cost_estimate=cost(5_000_000_000, 6 << 20), name="halo",
    )(m, below, above, weighted, lane, tile, own)
    parts = [parts[0]] + [lax.ppermute(parts[k], "mode", ring("mode", k)) for k in (1, 2, 3)]
    w_out16 = jnp.concatenate([w_out, jnp.zeros((7, 256), BF16)], axis=0)
    features_grad, *sums = pl.pallas_call(
        backward_kernel,
        out_shape=[shape((slots, 128), BF16)] + [shape((ROWS, T))] * 4, grid=(steps,),
        in_specs=[SMEM] + [full(9, QUARTER, T)] * 4
        + [rows_spec(128), rows_spec(256), rows_spec(256), full(128, 256), full(16, 256)],
        out_specs=[rows_spec(128)] + [full(ROWS, T)] * 4,
        scratch_shapes=[pltpu.VMEM((QUARTER, 16, T), BF16), pltpu.VMEM((SUM_ROWS, T), F32)],
        compiler_params=PARAMS, cost_estimate=cost(2_000_000_000, 9 << 20), name="backward",
    )(m, *parts, pair_features, hidden, slope, w_in, w_out16)
    share = sums[0]
    for k in (1, 2, 3):
        share = share + lax.ppermute(sums[k], "mode", ring("mode", k))
    line = [[g * 8 + k for k in range(8)] for g in range(8)]
    plane = [[k * 8 + g for k in range(8)] for g in range(8)]
    for groups in (line, plane):
        spread = jnp.broadcast_to(share[None], (8, ROWS, T))
        got = lax.all_to_all(spread, "slab", 0, 0, axis_index_groups=groups, tiled=True)
        share = jnp.sum(got, axis=0)
    pieces = [share] + [lax.ppermute(share, "mode", ring("mode", k)) for k in (1, 2, 3)]
    grad_w_in, grad_b_in, grad_w_out = pl.pallas_call(
        finish_kernel, out_shape=[shape((128, 256)), shape((1, 256)), shape((9, 256))],
        in_specs=[SMEM] + [VMEM] * 4, out_specs=[VMEM] * 3,
        scratch_shapes=[pltpu.VMEM((SUM_ROWS, T), F32)],
        compiler_params=PARAMS, name="finish",
    )(m, *pieces)
    return (features_grad, grad_w_in, grad_b_in.reshape(256), grad_w_out)


def solution(mesh):
    return jax.shard_map(
        shards,
        mesh=mesh,
        in_specs=(
            P("slab", None, "mode"),
            P("slab"),
            P("mode"),
            P("slab", None),
            P(("slab", "mode"), None),
            P(),
            P(),
            P(),
        ),
        out_specs=(P(("slab", "mode"), None), P(), P(), P()),
        check_vma=False,
    )
```

```python
import functools

import jax
import jax.numpy as jnp
from jax import lax
from jax.experimental import pallas as pl
from jax.experimental.pallas import tpu as pltpu
from jax.sharding import PartitionSpec as P

MASS_TABLE = (1.35, 2.94, 2.79, 2.95)
CLIP_NORM = 100.0
T = 128
ATOMS = 1280
RIM = 640
BLOCKS = ATOMS // T
REACH = RIM // T
GROUPS = ATOMS // 8
QUARTER = GROUPS // 4
F32, BF16 = jnp.float32, jnp.bfloat16
VMEM = pl.BlockSpec(memory_space=pltpu.VMEM)
SMEM = pl.BlockSpec(memory_space=pltpu.SMEM)
PARAMS = pltpu.CompilerParams(vmem_limit_bytes=40 << 20)


def nt_dot(x, y):
    return lax.dot_general(x, y, (((1,), (1,)), ((), ())), preferred_element_type=F32)


def tn_dot(x, y):
    return lax.dot_general(x, y, (((0,), (0,)), ((), ())), preferred_element_type=F32)


STRIP = 3 * T


def scale_kernel(eig, species, high, low):
    def half(base, out):
        for blk in range(REACH):
            rows = slice(base + blk * T, base + (blk + 1) * T)
            kind = species[:, rows]
            mass = jnp.full(kind.shape, MASS_TABLE[3], F32)
            for k in range(3):
                mass = jnp.where(kind == k, MASS_TABLE[k], mass)
            inv = jnp.broadcast_to(lax.rsqrt(mass), (T, T)).T
            inv = jnp.concatenate([inv, inv], axis=1)
            for a in range(3):
                at = blk * STRIP + a * T
                out[at:at + T, :] = (eig[a, rows, :].astype(F32) * inv).astype(BF16)

    half(RIM, high)
    half(0, low)


def fold_matrix():
    row = lax.broadcasted_iota(jnp.int32, (2 * T // 8, 2 * T), 0)
    col = lax.broadcasted_iota(jnp.int32, (2 * T // 8, 2 * T), 1)
    return (col // 8 == row).astype(BF16)


def pick(dense, per, local, a, b, at):
    place = local * 3 + b
    return dense[place // per, pl.ds(a * T + at, 8), (place % per) * T:(place % per + 1) * T]


def pipeline(jobs, weighted, lane_ref, tile_ref, dense, per, terms, with_self, pairs_of):
    width = per * T

    def multiply(job, out, c):
        i, rows, first, _, _ = job
        at = pl.ds(pl.multiple_of(first + c * width, T), width)
        out[c] = nt_dot(weighted[i], rows[at, :])

    def gather(job, src, step):
        i, _, _, first_tile, tiles = job
        found = []
        for half in range(2):
            at = pl.multiple_of(step * 16 + half * 8, 8)
            lane, where_tile = lane_ref[i, pl.ds(at, 8), :], tile_ref[i, pl.ds(at, 8), :]
            sums = [jnp.zeros((8, T), F32)] * 9
            for local in range(tiles):
                here = where_tile == first_tile + local
                for a in range(3):
                    for b in range(3):
                        got = jnp.take_along_axis(pick(src, per, local, a, b, at), lane, axis=1,
                                                  mode="promise_in_bounds")
                        sums[3 * a + b] = jnp.where(here, got, sums[3 * a + b])
            if with_self:
                mine = lax.broadcasted_iota(jnp.int32, (8, T), 0) + at
                live = where_tile >= 0
                for a in range(3):
                    for b in range(3):
                        got = jnp.take_along_axis(pick(src, per, i + REACH - first_tile, a, b, at), mine, axis=1,
                                                  mode="promise_in_bounds")
                        sums[3 * a + b] = jnp.where(live, sums[3 * a + b] - got, 0.0)
            found.append(sums)
        place = pl.ds(pl.multiple_of(i * T + step * 16, 16), 16)
        for c in range(9):
            terms[c, place, :] = jnp.concatenate([found[0][c], found[1][c]], axis=0).astype(BF16)

    def chunks(job):
        return -(-job[4] * 3 // per)

    for c in range(chunks(jobs[0])):
        multiply(jobs[0], dense[0], c)
    for k, job in enumerate(jobs):
        src, other = dense[k % 2], dense[(k + 1) % 2]
        ahead = chunks(jobs[k + 1]) if k + 1 < len(jobs) else 0
        pairs = pairs_of(job[4])
        turns = T // 16 // pairs
        each = -(-ahead // turns)

        def turn(step, carry, products, k=k, job=job, src=src, other=other, pairs=pairs):
            for c in range(products):
                multiply(jobs[k + 1], other, step * products + c)
            for p in range(pairs):
                gather(job, src, step * pairs + p)
            return carry

        full = ahead // each if each else 0
        left = ahead - full * each
        if full:
            lax.fori_loop(0, full, functools.partial(turn, products=each), 0)
        if left:
            for c in range(left):
                multiply(jobs[k + 1], other, full * each + c)
        if full < turns:
            lax.fori_loop(full, turns, functools.partial(turn, products=0), 0)


def own_kernel(high, low, mode_cot, nbr_t, out, weighted, lane_ref, tile_ref, stack, dense0, dense1, terms):
    row = lax.broadcasted_iota(jnp.int32, (T, T), 0)
    col = lax.broadcasted_iota(jnp.int32, (T, T), 1)
    diagonal = (row % 8) == (col // 16)
    cot = mode_cot[...]
    for blk in range(BLOCKS):
        n = nbr_t[:, blk * T:(blk + 1) * T].astype(F32)
        n = jnp.concatenate([n] * 8, axis=0).T.astype(jnp.int32)
        live = diagonal & (n < ATOMS + 2 * RIM)
        tile_ref[blk] = jnp.where(live, n >> 7, -1)
        lane_ref[blk] = n & (T - 1)
        src = low if blk < REACH else high
        s = src[blk % REACH * STRIP:(blk % REACH + 1) * STRIP, :]
        stack[blk * STRIP:(blk + 1) * STRIP, :] = s
        weighted[blk] = (s.astype(F32) * cot).astype(BF16)
    stack[BLOCKS * STRIP:, :] = jnp.zeros((STRIP, 256), BF16)
    jobs = []
    for i in range(BLOCKS):
        first, last = max(i - REACH, 0), min(i + REACH, BLOCKS - 1)
        jobs.append((i, stack, first * STRIP, first + REACH, last - first + 1))
    pipeline(jobs, weighted, lane_ref, tile_ref, (dense0, dense1), 6, terms, True, lambda tiles: 4)
    fold = fold_matrix()
    for h in range(BLOCKS // 2):
        for c in range(9):
            out[c, h * 32:(h + 1) * 32, :] = jnp.dot(
                fold, terms[c, h * 2 * T:(h + 1) * 2 * T, :], preferred_element_type=F32)


def halo_kernel(mode_index, below, above, weighted, lane_ref, tile_ref, own,
                out0, out1, out2, out3, dense0, dense1, terms, total):
    jobs = [(i, below, i * STRIP, i, REACH - i) for i in range(REACH)]
    jobs += [(i, above, 0, 3 * REACH, i - REACH + 1) for i in range(REACH, BLOCKS)]
    pipeline(jobs, weighted, lane_ref, tile_ref, (dense0, dense1), 3, terms, False, lambda tiles: 8)
    fold = fold_matrix()
    for h in range(BLOCKS // 2):
        for c in range(9):
            at = slice(h * 32, (h + 1) * 32)
            total[c, at, :] = own[c, at, :] + jnp.dot(
                fold, terms[c, h * 2 * T:(h + 1) * 2 * T, :], preferred_element_type=F32)
    m = mode_index[0]
    for k, out in enumerate((out0, out1, out2, out3)):
        q = lax.rem(m + k, 4)
        out[...] = total[:, pl.ds(pl.multiple_of(q * QUARTER, 8), QUARTER), :].astype(BF16)


CHUNK = 512


def forward_kernel(features, w_in, b_in, hidden, slope):
    pre = jnp.dot(features[...], w_in[...], preferred_element_type=F32) + b_in[...]
    sig = 1.0 / (1.0 + jnp.exp(-pre))
    hidden[...] = (pre * sig).astype(BF16)
    slope[...] = (sig * (1.0 + pre * (1.0 - sig))).astype(BF16)


def backward_kernel(mode_index, p0, p1, p2, p3, features, hidden, slope, w_in, w_out,
                    grad, g0, g1, g2, g3, cot, sums):
    step = pl.program_id(0)

    @pl.when(step == 0)
    def _():
        whole = sum(p[...].astype(F32) for p in (p0, p1, p2, p3))
        whole = jnp.concatenate([whole, jnp.zeros((7, QUARTER, T), F32)], axis=0)
        cot[...] = jnp.swapaxes(whole, 0, 1).astype(BF16)
        sums[...] = jnp.zeros_like(sums)

    per = CHUNK // T
    pair_cot = jnp.concatenate([cot[step * per + g] for g in range(per)], axis=1)
    pre_cot32 = tn_dot(pair_cot, w_out[...]) * slope[...].astype(F32)
    pre_cot = pre_cot32.astype(BF16)
    grad[...] = nt_dot(pre_cot, w_in[...]).astype(BF16)
    part_in = tn_dot(features[...], pre_cot)
    part_out = jnp.dot(pair_cot, hidden[...], preferred_element_type=F32)
    part_b = jnp.sum(pre_cot.astype(F32), axis=0, keepdims=True)
    part_b = jnp.concatenate([part_b, jnp.zeros((7, 256), F32)], axis=0)
    for h in range(2):
        cols = slice(h * T, (h + 1) * T)
        sums[h * 152:h * 152 + 128, :] += part_in[:, cols]
        sums[h * 152 + 128:h * 152 + 144, :] += part_out[:, cols]
        sums[h * 152 + 144:h * 152 + 152, :] += part_b[:, cols]

    @pl.when(step == pl.num_programs(0) - 1)
    def _():
        m = mode_index[0]
        for k, out in enumerate((g0, g1, g2, g3)):
            q = lax.rem(m + k, 4)
            out[...] = sums[pl.ds(pl.multiple_of(q * ROWS, 8), ROWS), :]


SUM_ROWS = 320
ROWS = SUM_ROWS // 4


def finish_kernel(mode_index, c0, c1, c2, c3, grad_w_in, grad_b_in, grad_w_out, whole):
    m = mode_index[0]
    for k, part in enumerate((c0, c1, c2, c3)):
        q = lax.rem(m + 4 - k, 4)
        whole[pl.ds(pl.multiple_of(q * ROWS, 8), ROWS), :] = part[...]
    both = []
    for start, rows in ((0, 128), (128, 9), (144, 1)):
        both.append(jnp.concatenate([whole[h * 152 + start:h * 152 + start + rows, :] for h in range(2)], axis=1))
    w, o, b = both
    norm_sq = jnp.sum(w * w) + jnp.sum(b * b) + jnp.sum(o * o)
    factor = jnp.minimum(1.0, CLIP_NORM / jnp.sqrt(jnp.broadcast_to(norm_sq + 1e-06, (1, 256))))
    grad_w_in[...] = w * factor
    grad_b_in[...] = b * factor
    grad_w_out[...] = o * factor


def shape(dims, dtype=F32):
    return jax.ShapeDtypeStruct(dims, dtype)


def cost(flops, moved):
    return pl.CostEstimate(flops=flops, bytes_accessed=moved, transcendentals=0)


def ring(axis, k):
    n = lax.axis_size(axis)
    return [(i, (i + k) % n) for i in range(n)]


def shards(eigvec, species, mode_cot, neighbours, pair_features, w_in, b_in, w_out):
    eig = jnp.transpose(eigvec, (1, 0, 2))
    m = lax.axis_index("mode").astype(jnp.int32).reshape(1)
    high, low = pl.pallas_call(
        scale_kernel, out_shape=[shape((REACH * STRIP, 256), BF16)] * 2,
        in_specs=[VMEM] * 2, out_specs=[VMEM] * 2, compiler_params=PARAMS,
        cost_estimate=cost(1 << 20, 4 << 20), name="scale",
    )(eig, species.reshape(1, ATOMS))
    below = lax.ppermute(high, "slab", ring("slab", 1))
    above = lax.ppermute(low, "slab", ring("slab", lax.axis_size("slab") - 1))
    own, weighted, lane, tile = pl.pallas_call(
        own_kernel,
        out_shape=[shape((9, GROUPS, T)), shape((BLOCKS, 3 * T, 256), BF16),
                   shape((BLOCKS, T, T), jnp.int32), shape((BLOCKS, T, T), jnp.int32)],
        in_specs=[VMEM] * 4, out_specs=[VMEM] * 4,
        scratch_shapes=[pltpu.VMEM(((BLOCKS + 1) * STRIP, 256), BF16)]
        + [pltpu.VMEM((5, STRIP, 6 * T), F32)] * 2 + [pltpu.VMEM((9, ATOMS, T), BF16)],
        compiler_params=PARAMS, cost_estimate=cost(12_000_000_000, 6 << 20), name="own",
    )(high, low, mode_cot.reshape(1, 256), neighbours.T)
    slots = pair_features.shape[0]
    steps = slots // CHUNK
    rows_spec = lambda width: pl.BlockSpec((CHUNK, width), lambda s: (s, 0))
    full = lambda *dims: pl.BlockSpec(dims, lambda s: (0,) * len(dims))
    hidden, slope = pl.pallas_call(
        forward_kernel, out_shape=[shape((slots, 256), BF16)] * 2, grid=(steps,),
        in_specs=[rows_spec(128), full(128, 256), full(1, 256)], out_specs=[rows_spec(256)] * 2,
        compiler_params=PARAMS, cost_estimate=cost(4_000_000_000, 7 << 20), name="forward",
    )(pair_features, w_in, b_in.reshape(1, 256))
    parts = pl.pallas_call(
        halo_kernel, out_shape=[shape((9, QUARTER, T), BF16)] * 4,
        in_specs=[SMEM] + [VMEM] * 6, out_specs=[VMEM] * 4,
        scratch_shapes=[pltpu.VMEM((REACH, STRIP, 3 * T), F32)] * 2
        + [pltpu.VMEM((9, ATOMS, T), BF16), pltpu.VMEM((9, GROUPS, T), F32)],
        compiler_params=PARAMS, cost_estimate=cost(5_000_000_000, 6 << 20), name="halo",
    )(m, below, above, weighted, lane, tile, own)
    parts = [parts[0]] + [lax.ppermute(parts[k], "mode", ring("mode", k)) for k in (1, 2, 3)]
    w_out16 = jnp.concatenate([w_out, jnp.zeros((7, 256), BF16)], axis=0)
    features_grad, *sums = pl.pallas_call(
        backward_kernel,
        out_shape=[shape((slots, 128), BF16)] + [shape((ROWS, T))] * 4, grid=(steps,),
        in_specs=[SMEM] + [full(9, QUARTER, T)] * 4
        + [rows_spec(128), rows_spec(256), rows_spec(256), full(128, 256), full(16, 256)],
        out_specs=[rows_spec(128)] + [full(ROWS, T)] * 4,
        scratch_shapes=[pltpu.VMEM((QUARTER, 16, T), BF16), pltpu.VMEM((SUM_ROWS, T), F32)],
        compiler_params=PARAMS, cost_estimate=cost(2_000_000_000, 9 << 20), name="backward",
    )(m, *parts, pair_features, hidden, slope, w_in, w_out16)
    share = sums[0]
    for k in (1, 2, 3):
        share = share + lax.ppermute(sums[k], "mode", ring("mode", k))
    line = [[g * 8 + k for k in range(8)] for g in range(8)]
    plane = [[k * 8 + g for k in range(8)] for g in range(8)]
    for groups in (line, plane):
        spread = jnp.broadcast_to(share.astype(BF16)[None], (8, ROWS, T))
        got = lax.all_to_all(spread, "slab", 0, 0, axis_index_groups=groups, tiled=True)
        share = jnp.sum(got.astype(F32), axis=0)
    pieces = [share] + [lax.ppermute(share, "mode", ring("mode", k)) for k in (1, 2, 3)]
    grad_w_in, grad_b_in, grad_w_out = pl.pallas_call(
        finish_kernel, out_shape=[shape((128, 256)), shape((1, 256)), shape((9, 256))],
        in_specs=[SMEM] + [VMEM] * 4, out_specs=[VMEM] * 3,
        scratch_shapes=[pltpu.VMEM((SUM_ROWS, T), F32)],
        compiler_params=PARAMS, name="finish",
    )(m, *pieces)
    return (features_grad, grad_w_in, grad_b_in.reshape(256), grad_w_out)


def solution(mesh):
    return jax.shard_map(
        shards,
        mesh=mesh,
        in_specs=(
            P("slab", None, "mode"),
            P("slab"),
            P("mode"),
            P("slab", None),
            P(("slab", "mode"), None),
            P(),
            P(),
            P(),
        ),
        out_specs=(P(("slab", "mode"), None), P(), P(), P()),
        check_vma=False,
    )
```

```python
import functools

import jax
import jax.numpy as jnp
from jax import lax
from jax.experimental import pallas as pl
from jax.experimental.pallas import tpu as pltpu
from jax.sharding import PartitionSpec as P

MASS_TABLE = (1.35, 2.94, 2.79, 2.95)
CLIP_NORM = 100.0
T = 128
ATOMS = 1280
RIM = 640
BLOCKS = ATOMS // T
REACH = RIM // T
GROUPS = ATOMS // 8
QUARTER = GROUPS // 4
F32, BF16 = jnp.float32, jnp.bfloat16
VMEM = pl.BlockSpec(memory_space=pltpu.VMEM)
SMEM = pl.BlockSpec(memory_space=pltpu.SMEM)
PARAMS = pltpu.CompilerParams(vmem_limit_bytes=40 << 20)


def nt_dot(x, y):
    return lax.dot_general(x, y, (((1,), (1,)), ((), ())), preferred_element_type=F32)


def tn_dot(x, y):
    return lax.dot_general(x, y, (((0,), (0,)), ((), ())), preferred_element_type=F32)


STRIP = 3 * T


def scale_kernel(eig, species, high, low):
    def half(base, out):
        for blk in range(REACH):
            rows = slice(base + blk * T, base + (blk + 1) * T)
            kind = species[rows].reshape(1, T)
            mass = jnp.full(kind.shape, MASS_TABLE[3], F32)
            for k in range(3):
                mass = jnp.where(kind == k, MASS_TABLE[k], mass)
            inv = jnp.broadcast_to(lax.rsqrt(mass), (T, T)).T
            inv = jnp.concatenate([inv, inv], axis=1)
            for a in range(3):
                at = blk * STRIP + a * T
                out[at:at + T, :] = (eig[a, rows, :].astype(F32) * inv).astype(BF16)

    half(RIM, high)
    half(0, low)


def fold_matrix():
    row = lax.broadcasted_iota(jnp.int32, (2 * T // 8, 2 * T), 0)
    col = lax.broadcasted_iota(jnp.int32, (2 * T // 8, 2 * T), 1)
    return (col // 8 == row).astype(BF16)


def pick(dense, per, local, a, b, at):
    place = local * 3 + b
    return dense[place // per, pl.ds(a * T + at, 8), (place % per) * T:(place % per + 1) * T]


def pipeline(jobs, weighted, lane_ref, tile_ref, dense, per, terms, with_self, pairs_of):
    width = per * T

    def multiply(job, out, c):
        i, rows, first, _, _ = job
        at = pl.ds(pl.multiple_of(first + c * width, T), width)
        out[c] = nt_dot(weighted[i], rows[at, :])

    def gather(job, src, step):
        i, _, _, first_tile, tiles = job
        found = []
        for half in range(2):
            at = pl.multiple_of(step * 16 + half * 8, 8)
            lane, where_tile = lane_ref[i, pl.ds(at, 8), :], tile_ref[i, pl.ds(at, 8), :]
            sums = [jnp.zeros((8, T), F32)] * 9
            for local in range(tiles):
                here = where_tile == first_tile + local
                for a in range(3):
                    for b in range(3):
                        got = jnp.take_along_axis(pick(src, per, local, a, b, at), lane, axis=1,
                                                  mode="promise_in_bounds")
                        sums[3 * a + b] = jnp.where(here, got, sums[3 * a + b])
            if with_self:
                mine = lax.broadcasted_iota(jnp.int32, (8, T), 0) + at
                live = where_tile >= 0
                for a in range(3):
                    for b in range(3):
                        got = jnp.take_along_axis(pick(src, per, i + REACH - first_tile, a, b, at), mine, axis=1,
                                                  mode="promise_in_bounds")
                        sums[3 * a + b] = jnp.where(live, sums[3 * a + b] - got, 0.0)
            found.append(sums)
        place = pl.ds(pl.multiple_of(i * T + step * 16, 16), 16)
        for c in range(9):
            terms[c, place, :] = jnp.concatenate([found[0][c], found[1][c]], axis=0).astype(BF16)

    def chunks(job):
        return -(-job[4] * 3 // per)

    for c in range(chunks(jobs[0])):
        multiply(jobs[0], dense[0], c)
    for k, job in enumerate(jobs):
        src, other = dense[k % 2], dense[(k + 1) % 2]
        ahead = chunks(jobs[k + 1]) if k + 1 < len(jobs) else 0
        pairs = pairs_of(job[4])
        turns = T // 16 // pairs
        each = -(-ahead // turns)

        def turn(step, carry, products, k=k, job=job, src=src, other=other, pairs=pairs):
            for c in range(products):
                multiply(jobs[k + 1], other, step * products + c)
            for p in range(pairs):
                gather(job, src, step * pairs + p)
            return carry

        full = ahead // each if each else 0
        left = ahead - full * each
        if full:
            lax.fori_loop(0, full, functools.partial(turn, products=each), 0)
        if left:
            for c in range(left):
                multiply(jobs[k + 1], other, full * each + c)
        if full < turns:
            lax.fori_loop(full, turns, functools.partial(turn, products=0), 0)


def own_kernel(high, low, mode_cot, nbr_t, out, weighted, lane_ref, tile_ref, stack, dense0, dense1, terms):
    row = lax.broadcasted_iota(jnp.int32, (T, T), 0)
    col = lax.broadcasted_iota(jnp.int32, (T, T), 1)
    diagonal = (row % 8) == (col // 16)
    cot = mode_cot[...]
    for blk in range(BLOCKS):
        n = nbr_t[:, blk * T:(blk + 1) * T].astype(F32)
        n = jnp.concatenate([n] * 8, axis=0).T.astype(jnp.int32)
        live = diagonal & (n < ATOMS + 2 * RIM)
        tile_ref[blk] = jnp.where(live, n >> 7, -1)
        lane_ref[blk] = n & (T - 1)
        src = low if blk < REACH else high
        s = src[blk % REACH * STRIP:(blk % REACH + 1) * STRIP, :]
        stack[blk * STRIP:(blk + 1) * STRIP, :] = s
        weighted[blk] = (s.astype(F32) * cot).astype(BF16)
    stack[BLOCKS * STRIP:, :] = jnp.zeros((STRIP, 256), BF16)
    jobs = []
    for i in range(BLOCKS):
        first, last = max(i - REACH, 0), min(i + REACH, BLOCKS - 1)
        jobs.append((i, stack, first * STRIP, first + REACH, last - first + 1))
    pipeline(jobs, weighted, lane_ref, tile_ref, (dense0, dense1), 6, terms, True, lambda tiles: 8)
    fold = fold_matrix()
    for h in range(BLOCKS // 2):
        for c in range(9):
            out[c, h * 32:(h + 1) * 32, :] = jnp.dot(
                fold, terms[c, h * 2 * T:(h + 1) * 2 * T, :], preferred_element_type=F32)


def halo_kernel(mode_index, below, above, weighted, lane_ref, tile_ref, own, _after,
                out0, out1, out2, out3, dense0, dense1, terms, total):
    jobs = [(i, below, i * STRIP, i, REACH - i) for i in range(REACH)]
    jobs += [(i, above, 0, 3 * REACH, i - REACH + 1) for i in range(REACH, BLOCKS)]
    pipeline(jobs, weighted, lane_ref, tile_ref, (dense0, dense1), 3, terms, False, lambda tiles: 8)
    fold = fold_matrix()
    for h in range(BLOCKS // 2):
        for c in range(9):
            at = slice(h * 32, (h + 1) * 32)
            total[c, at, :] = own[c, at, :] + jnp.dot(
                fold, terms[c, h * 2 * T:(h + 1) * 2 * T, :], preferred_element_type=F32)
    m = mode_index[0]
    for k, out in enumerate((out0, out1, out2, out3)):
        q = lax.rem(m + k, 4)
        out[...] = total[:, pl.ds(pl.multiple_of(q * QUARTER, 8), QUARTER), :].astype(BF16)


CHUNK = 512
EXT = 144


def forward_kernel(features, w_in, b_in, hidden, slope, turned):
    x = features[...]
    pre = jnp.dot(x, w_in[...], preferred_element_type=F32) + b_in[...]
    sig = 1.0 / (1.0 + jnp.exp(-pre))
    hidden[...] = (pre * sig).astype(BF16)
    slope[...] = (sig * (1.0 + pre * (1.0 - sig))).astype(BF16)
    turned[0:128, :] = x.T
    row = lax.broadcasted_iota(jnp.int32, (EXT - 128, CHUNK), 0)
    turned[128:EXT, :] = (row == 0).astype(BF16)


def gradient_kernel(mode_index, p0, p1, p2, p3, turned, hidden, slope, w_out,
                    pre_cot, g0, g1, g2, g3, cot, sums):
    whole = sum(p[...].astype(F32) for p in (p0, p1, p2, p3))
    whole = jnp.concatenate([whole, jnp.zeros((7, QUARTER, T), F32)], axis=0)
    cot[...] = jnp.swapaxes(whole, 0, 1).astype(BF16)
    sums[...] = jnp.zeros_like(sums)
    w_out16 = jnp.concatenate([w_out[...].astype(F32), jnp.zeros((7, 256), F32)], axis=0).astype(BF16)
    per = CHUNK // T
    total_in, total_out = jnp.zeros((EXT, 256), F32), jnp.zeros((16, 256), F32)
    for step in range(hidden.shape[0] // CHUNK):
        rows = slice(step * CHUNK, (step + 1) * CHUNK)
        pair_cot = jnp.concatenate([cot[step * per + g] for g in range(per)], axis=1)
        part = (tn_dot(pair_cot, w_out16) * slope[rows, :].astype(F32)).astype(BF16)
        pre_cot[rows, :] = part
        total_in += jnp.dot(turned[:, rows], part, preferred_element_type=F32)
        total_out += jnp.dot(pair_cot, hidden[rows, :], preferred_element_type=F32)
    for h in range(2):
        cols = slice(h * T, (h + 1) * T)
        sums[h * 152:h * 152 + 128, :] = total_in[0:128, cols]
        sums[h * 152 + 128:h * 152 + 144, :] = total_out[:, cols]
        sums[h * 152 + 144:h * 152 + 152, :] = total_in[128:136, cols]
    m = mode_index[0]
    for k, out in enumerate((g0, g1, g2, g3)):
        q = lax.rem(m + k, 4)
        out[...] = sums[pl.ds(pl.multiple_of(q * ROWS, 8), ROWS), :]


def features_kernel(pre_cot, w_in, grad):
    grad[...] = nt_dot(pre_cot[...], w_in[...]).astype(BF16)


SUM_ROWS = 320
ROWS = SUM_ROWS // 4


def finish_kernel(mode_index, c0, c1, c2, c3, grad_w_in, grad_b_in, grad_w_out, whole):
    m = mode_index[0]
    for k, part in enumerate((c0, c1, c2, c3)):
        q = lax.rem(m + 4 - k, 4)
        whole[pl.ds(pl.multiple_of(q * ROWS, 8), ROWS), :] = part[...]
    both = []
    for start, rows in ((0, 128), (128, 9), (144, 1)):
        both.append(jnp.concatenate([whole[h * 152 + start:h * 152 + start + rows, :] for h in range(2)], axis=1))
    w, o, b = both
    norm_sq = jnp.sum(w * w) + jnp.sum(b * b) + jnp.sum(o * o)
    factor = jnp.minimum(1.0, CLIP_NORM / jnp.sqrt(jnp.broadcast_to(norm_sq + 1e-06, (1, 256))))
    grad_w_in[...] = w * factor
    grad_b_in[...] = b * factor
    grad_w_out[...] = o * factor


def shape(dims, dtype=F32):
    return jax.ShapeDtypeStruct(dims, dtype)


def cost(flops, moved):
    return pl.CostEstimate(flops=flops, bytes_accessed=moved, transcendentals=0)


def ring(axis, k):
    n = lax.axis_size(axis)
    return [(i, (i + k) % n) for i in range(n)]


def shards(eigvec, species, mode_cot, neighbours, pair_features, w_in, b_in, w_out):
    eig = jnp.transpose(eigvec, (1, 0, 2))
    m = lax.axis_index("mode").astype(jnp.int32).reshape(1)
    high, low = pl.pallas_call(
        scale_kernel, out_shape=[shape((REACH * STRIP, 256), BF16)] * 2,
        in_specs=[VMEM] * 2, out_specs=[VMEM] * 2, compiler_params=PARAMS,
        cost_estimate=cost(1 << 20, 4 << 20), name="scale",
    )(eig, species)
    below = lax.ppermute(high, "slab", ring("slab", 1))
    above = lax.ppermute(low, "slab", ring("slab", lax.axis_size("slab") - 1))
    own, weighted, lane, tile = pl.pallas_call(
        own_kernel,
        out_shape=[shape((9, GROUPS, T)), shape((BLOCKS, 3 * T, 256), BF16),
                   shape((BLOCKS, T, T), jnp.int32), shape((BLOCKS, T, T), jnp.int32)],
        in_specs=[VMEM] * 4, out_specs=[VMEM] * 4,
        scratch_shapes=[pltpu.VMEM(((BLOCKS + 1) * STRIP, 256), BF16)]
        + [pltpu.VMEM((5, STRIP, 6 * T), F32)] * 2 + [pltpu.VMEM((9, ATOMS, T), BF16)],
        compiler_params=PARAMS, cost_estimate=cost(12_000_000_000, 6 << 20), name="own",
    )(high, low, mode_cot.reshape(1, 256), neighbours.T)
    slots = pair_features.shape[0]
    steps = slots // CHUNK
    rows_spec = lambda width: pl.BlockSpec((CHUNK, width), lambda s: (s, 0))
    full = lambda *dims: pl.BlockSpec(dims, lambda s: (0,) * len(dims))
    hidden, slope, turned = pl.pallas_call(
        forward_kernel, out_shape=[shape((slots, 256), BF16)] * 2 + [shape((EXT, slots), BF16)], grid=(steps,),
        in_specs=[rows_spec(128), full(128, 256), full(1, 256)],
        out_specs=[rows_spec(256)] * 2 + [pl.BlockSpec((EXT, CHUNK), lambda s: (0, s))],
        compiler_params=PARAMS, cost_estimate=cost(4_000_000_000, 8 << 20), name="forward",
    )(pair_features, w_in, b_in.reshape(1, 256))
    parts = pl.pallas_call(
        halo_kernel, out_shape=[shape((9, QUARTER, T), BF16)] * 4,
        in_specs=[SMEM] + [VMEM] * 6 + [pl.BlockSpec(memory_space=pl.ANY)], out_specs=[VMEM] * 4,
        scratch_shapes=[pltpu.VMEM((REACH, STRIP, 3 * T), F32)] * 2
        + [pltpu.VMEM((9, ATOMS, T), BF16), pltpu.VMEM((9, GROUPS, T), F32)],
        compiler_params=PARAMS, cost_estimate=cost(5_000_000_000, 6 << 20), name="halo",
    )(m, below, above, weighted, lane, tile, own, turned)
    parts = [parts[0]] + [lax.ppermute(parts[k], "mode", ring("mode", k)) for k in (1, 2, 3)]
    pre_cot, *sums = pl.pallas_call(
        gradient_kernel,
        out_shape=[shape((slots, 256), BF16)] + [shape((ROWS, T))] * 4,
        in_specs=[SMEM] + [VMEM] * 8, out_specs=[VMEM] * 5,
        scratch_shapes=[pltpu.VMEM((QUARTER, 16, T), BF16), pltpu.VMEM((SUM_ROWS, T), F32)],
        compiler_params=PARAMS, cost_estimate=cost(2_000_000_000, 9 << 20), name="gradient",
    )(m, *parts, turned, hidden, slope, w_out)
    features_grad = pl.pallas_call(
        features_kernel, out_shape=shape((slots, 128), BF16), grid=(steps // 2,),
        in_specs=[pl.BlockSpec((2 * CHUNK, 256), lambda s: (s, 0)), full(128, 256)],
        out_specs=pl.BlockSpec((2 * CHUNK, 128), lambda s: (s, 0)),
        compiler_params=PARAMS, cost_estimate=cost(2_000_000_000, 5 << 20), name="features",
    )(pre_cot, w_in)
    share = sums[0]
    for k in (1, 2, 3):
        share = share + lax.ppermute(sums[k], "mode", ring("mode", k))
    line = [[g * 8 + k for k in range(8)] for g in range(8)]
    plane = [[k * 8 + g for k in range(8)] for g in range(8)]
    for groups in (line, plane):
        spread = jnp.broadcast_to(share.astype(BF16)[None], (8, ROWS, T))
        got = lax.all_to_all(spread, "slab", 0, 0, axis_index_groups=groups, tiled=True)
        share = jnp.sum(got.astype(F32), axis=0)
    pieces = [share] + [lax.ppermute(share, "mode", ring("mode", k)) for k in (1, 2, 3)]
    grad_w_in, grad_b_in, grad_w_out = pl.pallas_call(
        finish_kernel, out_shape=[shape((128, 256)), shape((1, 256)), shape((9, 256))],
        in_specs=[SMEM] + [VMEM] * 4, out_specs=[VMEM] * 3,
        scratch_shapes=[pltpu.VMEM((SUM_ROWS, T), F32)],
        compiler_params=PARAMS, name="finish",
    )(m, *pieces)
    return (features_grad, grad_w_in, grad_b_in.reshape(256), grad_w_out)


def solution(mesh):
    return jax.shard_map(
        shards,
        mesh=mesh,
        in_specs=(
            P("slab", None, "mode"),
            P("slab"),
            P("mode"),
            P("slab", None),
            P(("slab", "mode"), None),
            P(),
            P(),
            P(),
        ),
        out_specs=(P(("slab", "mode"), None), P(), P(), P()),
        check_vma=False,
    )
```

```python
import functools

import jax
import jax.numpy as jnp
from jax import lax
from jax.experimental import pallas as pl
from jax.experimental.pallas import tpu as pltpu
from jax.sharding import PartitionSpec as P

MASS_TABLE = (1.35, 2.94, 2.79, 2.95)
CLIP_NORM = 100.0
T = 128
ATOMS = 1280
RIM = 640
BLOCKS = ATOMS // T
REACH = RIM // T
GROUPS = ATOMS // 8
QUARTER = GROUPS // 4
F32, BF16 = jnp.float32, jnp.bfloat16
VMEM = pl.BlockSpec(memory_space=pltpu.VMEM)
SMEM = pl.BlockSpec(memory_space=pltpu.SMEM)
PARAMS = pltpu.CompilerParams(vmem_limit_bytes=40 << 20)


def nt_dot(x, y):
    return lax.dot_general(x, y, (((1,), (1,)), ((), ())), preferred_element_type=F32)


def tn_dot(x, y):
    return lax.dot_general(x, y, (((0,), (0,)), ((), ())), preferred_element_type=F32)


STRIP = 3 * T


NEAR = 3


def scale_kernel(eig, species, high_near, high_far, low_near, low_far):
    order = [blk for t in range(REACH) for blk in (BLOCKS - 1 - t, t)]
    for blk in order:
        rows = slice(blk * T, (blk + 1) * T)
        kind = species[rows].reshape(1, T)
        mass = jnp.full(kind.shape, MASS_TABLE[3], F32)
        for k in range(3):
            mass = jnp.where(kind == k, MASS_TABLE[k], mass)
        inv = jnp.broadcast_to(lax.rsqrt(mass), (T, T)).T
        inv = jnp.concatenate([inv, inv], axis=1)
        out, tile = place_of(blk, high_near, high_far, low_near, low_far)
        for a in range(3):
            at = tile * STRIP + a * T
            out[at:at + T, :] = (eig[a, rows, :].astype(F32) * inv).astype(BF16)


def place_of(blk, high_near, high_far, low_near, low_far):
    if blk < NEAR:
        return low_near, blk
    if blk < REACH:
        return low_far, blk - NEAR
    if blk < BLOCKS - NEAR:
        return high_far, blk - REACH
    return high_near, blk - (BLOCKS - NEAR)


def fold_matrix():
    row = lax.broadcasted_iota(jnp.int32, (2 * T // 8, 2 * T), 0)
    col = lax.broadcasted_iota(jnp.int32, (2 * T // 8, 2 * T), 1)
    return (col // 8 == row).astype(BF16)


def pick(dense, local, a, b, at):
    place = (local * 3 + b) * T
    return dense[a * T + at:a * T + at + 16, place:place + T]


def lane_gather(values, lane):
    numbers = lax.GatherDimensionNumbers(
        offset_dims=(), collapsed_slice_dims=(1,), start_index_map=(1,),
        operand_batching_dims=(0,), start_indices_batching_dims=(0,))
    return lax.gather(values, lane[..., None], numbers, slice_sizes=(1, 1),
                      mode=lax.GatherScatterMode.PROMISE_IN_BOUNDS)


def pipeline(jobs, weighted, lane_ref, tile_ref, dense, terms, with_self):
    def multiply(job, out):
        i, rows, first, _, tiles = job
        left = weighted[i]
        for start in range(0, tiles * STRIP, 2 * STRIP):
            stop = min(start + 2 * STRIP, tiles * STRIP)
            out[:, start:stop] = nt_dot(left, rows[first + start:first + stop, :]).astype(BF16)

    def gather(job, src, at):
        i, _, _, first_tile, tiles = job
        lane, where_tile = lane_ref[i, at:at + 16, :], tile_ref[i, at:at + 16, :]
        sums = [jnp.zeros((16, T), BF16)] * 9
        for local in range(tiles):
            here = where_tile == jnp.int16(first_tile + local)
            for a in range(3):
                for b in range(3):
                    got = lane_gather(pick(src, local, a, b, at), lane)
                    sums[3 * a + b] = jnp.where(here, got, sums[3 * a + b])
        if with_self:
            mine = (lax.broadcasted_iota(jnp.int32, (16, T), 0) + at).astype(jnp.int16)
            live = where_tile.astype(jnp.int32) >= 0
            for a in range(3):
                for b in range(3):
                    got = lane_gather(pick(src, i + REACH - first_tile, a, b, at), mine)
                    term = sums[3 * a + b].astype(F32) - got.astype(F32)
                    sums[3 * a + b] = jnp.where(live, term, 0.0).astype(BF16)
        for c in range(9):
            terms[c, i * T + at:i * T + at + 16, :] = sums[c]

    multiply(jobs[0], dense[0])
    for k, job in enumerate(jobs):

        def turn(step, carry, k=k, job=job):
            if k + 1 < len(jobs):
                multiply(jobs[k + 1], dense[(k + 1) % 2])
            for at in range(0, T, 16):
                gather(job, dense[k % 2], at)
            return carry

        turn(0, 0)


def own_kernel(high_near, high_far, low_near, low_far, mode_cot, nbr_t, out, weighted, lane_ref, tile_ref, stack, dense0, dense1, terms):
    row = lax.broadcasted_iota(jnp.int32, (T, T), 0)
    col = lax.broadcasted_iota(jnp.int32, (T, T), 1)
    diagonal = (row % 8) == (col // 16)
    cot = mode_cot[...]
    for blk in range(BLOCKS):
        n = nbr_t[:, blk * T:(blk + 1) * T].astype(F32)
        n = jnp.concatenate([n] * 8, axis=0).T.astype(jnp.int32)
        live = diagonal & (n < ATOMS + 2 * RIM)
        tile_ref[blk] = jnp.where(live, n >> 7, -1).astype(jnp.int16)
        lane_ref[blk] = (n & (T - 1)).astype(jnp.int16)
        src, tile = place_of(blk, high_near, high_far, low_near, low_far)
        s = src[tile * STRIP:(tile + 1) * STRIP, :]
        stack[blk * STRIP:(blk + 1) * STRIP, :] = s
        weighted[blk] = (s.astype(F32) * cot).astype(BF16)
    jobs = []
    for i in range(BLOCKS):
        first, last = max(i - REACH, 0), min(i + REACH, BLOCKS - 1)
        jobs.append((i, stack, first * STRIP, first + REACH, last - first + 1))
    pipeline(jobs, weighted, lane_ref, tile_ref, (dense0, dense1), terms, True)
    fold = fold_matrix()
    for h in range(BLOCKS // 2):
        for c in range(9):
            out[c, h * 32:(h + 1) * 32, :] = jnp.dot(
                fold, terms[c, h * 2 * T:(h + 1) * 2 * T, :], preferred_element_type=F32)


def near_kernel(below, above, weighted, lane_ref, tile_ref, own, total, dense0, dense1, terms):
    skip = REACH - NEAR
    jobs = []
    for i in reversed(range(REACH)):
        first = max(i, skip)
        jobs.append((i, below, (first - skip) * STRIP, first, REACH - first))
    for i in reversed(range(REACH, BLOCKS)):
        jobs.append((i, above, 0, 3 * REACH, min(i - REACH + 1, NEAR)))
    pipeline(jobs, weighted, lane_ref, tile_ref, (dense0, dense1), terms, False)
    fold = fold_matrix()
    for h in range(BLOCKS // 2):
        for c in range(9):
            at = slice(h * 32, (h + 1) * 32)
            total[c, at, :] = own[c, at, :] + jnp.dot(
                fold, terms[c, h * 2 * T:(h + 1) * 2 * T, :], preferred_element_type=F32)


def far_kernel(mode_index, below, above, weighted, lane_ref, tile_ref, before, _after,
               out0, out1, out2, out3, dense0, dense1, terms, total):
    skip = REACH - NEAR
    jobs = [(i, below, i * STRIP, i, skip - i) for i in reversed(range(skip))]
    jobs += [(i, above, 0, 3 * REACH + NEAR, i - REACH - NEAR + 1) for i in range(REACH + NEAR, BLOCKS)]
    pipeline(jobs, weighted, lane_ref, tile_ref, (dense0, dense1), terms, False)
    total[...] = before[...]
    fold = fold_matrix()
    for h in (0, BLOCKS // 2 - 1):
        for c in range(9):
            at = slice(h * 32, (h + 1) * 32)
            total[c, at, :] += jnp.dot(
                fold, terms[c, h * 2 * T:(h + 1) * 2 * T, :], preferred_element_type=F32)
    m = mode_index[0]
    for k, out in enumerate((out0, out1, out2, out3)):
        q = lax.rem(m + k, 4)
        out[...] = total[:, pl.ds(pl.multiple_of(q * QUARTER, 8), QUARTER), :].astype(BF16)


CHUNK = 512
EXT = 144


def forward_kernel(features, w_in, b_in, _after, hidden, slope, turned):
    x = features[...]
    pre = jnp.dot(x, w_in[...], preferred_element_type=F32) + b_in[...]
    sig = 1.0 / (1.0 + jnp.exp(-pre))
    hidden[...] = (pre * sig).astype(BF16)
    slope[...] = (sig * (1.0 + pre * (1.0 - sig))).astype(BF16)
    turned[0:128, :] = x.T
    row = lax.broadcasted_iota(jnp.int32, (EXT - 128, CHUNK), 0)
    turned[128:EXT, :] = (row == 0).astype(BF16)


def gradient_kernel(mode_index, p0, p1, p2, p3, turned, hidden, slope, w_out,
                    pre_cot, g0, g1, g2, g3, cot, sums):
    whole = sum(p[...].astype(F32) for p in (p0, p1, p2, p3))
    whole = jnp.concatenate([whole, jnp.zeros((7, QUARTER, T), F32)], axis=0)
    cot[...] = jnp.swapaxes(whole, 0, 1).astype(BF16)
    sums[...] = jnp.zeros_like(sums)
    w_out16 = jnp.concatenate([w_out[...].astype(F32), jnp.zeros((7, 256), F32)], axis=0).astype(BF16)
    per = CHUNK // T
    total_in, total_out = jnp.zeros((EXT, 256), F32), jnp.zeros((16, 256), F32)
    for step in range(hidden.shape[0] // CHUNK):
        rows = slice(step * CHUNK, (step + 1) * CHUNK)
        pair_cot = jnp.concatenate([cot[step * per + g] for g in range(per)], axis=1)
        part = (tn_dot(pair_cot, w_out16) * slope[rows, :].astype(F32)).astype(BF16)
        pre_cot[rows, :] = part
        total_in += jnp.dot(turned[:, rows], part, preferred_element_type=F32)
        total_out += jnp.dot(pair_cot, hidden[rows, :], preferred_element_type=F32)
    for h in range(2):
        cols = slice(h * T, (h + 1) * T)
        sums[h * 152:h * 152 + 128, :] = total_in[0:128, cols]
        sums[h * 152 + 128:h * 152 + 144, :] = total_out[:, cols]
        sums[h * 152 + 144:h * 152 + 152, :] = total_in[128:136, cols]
    m = mode_index[0]
    for k, out in enumerate((g0, g1, g2, g3)):
        q = lax.rem(m + k, 4)
        out[...] = sums[pl.ds(pl.multiple_of(q * ROWS, 8), ROWS), :]


def features_kernel(pre_cot, w_in, grad):
    grad[...] = nt_dot(pre_cot[...], w_in[...]).astype(BF16)


SUM_ROWS = 320
ROWS = SUM_ROWS // 4


def finish_kernel(mode_index, c0, c1, c2, c3, grad_w_in, grad_b_in, grad_w_out, whole):
    m = mode_index[0]
    for k, part in enumerate((c0, c1, c2, c3)):
        q = lax.rem(m + 4 - k, 4)
        whole[pl.ds(pl.multiple_of(q * ROWS, 8), ROWS), :] = part[...]
    both = []
    for start, rows in ((0, 128), (128, 9), (144, 1)):
        both.append(jnp.concatenate([whole[h * 152 + start:h * 152 + start + rows, :] for h in range(2)], axis=1))
    w, o, b = both
    norm_sq = jnp.sum(w * w) + jnp.sum(b * b) + jnp.sum(o * o)
    factor = jnp.minimum(1.0, CLIP_NORM / jnp.sqrt(jnp.broadcast_to(norm_sq + 1e-06, (1, 256))))
    grad_w_in[...] = w * factor
    grad_b_in[...] = b * factor
    grad_w_out[...] = o * factor


def shape(dims, dtype=F32):
    return jax.ShapeDtypeStruct(dims, dtype)


def cost(flops, moved):
    return pl.CostEstimate(flops=flops, bytes_accessed=moved, transcendentals=0)


def ring(axis, k):
    n = lax.axis_size(axis)
    return [(i, (i + k) % n) for i in range(n)]


def shards(eigvec, species, mode_cot, neighbours, pair_features, w_in, b_in, w_out):
    eig = jnp.transpose(eigvec, (1, 0, 2))
    m = lax.axis_index("mode").astype(jnp.int32).reshape(1)
    near, far = NEAR * STRIP, (REACH - NEAR) * STRIP
    anywhere = pl.BlockSpec(memory_space=pl.ANY)
    halves = pl.pallas_call(
        scale_kernel, out_shape=[shape((near, 256), BF16), shape((far, 256), BF16)] * 2,
        in_specs=[VMEM] * 2, out_specs=[VMEM] * 4,
        compiler_params=PARAMS, cost_estimate=cost(1 << 20, 4 << 20), name="scale",
    )(eig, species)
    high_near, high_far, low_near, low_far = halves
    up, down = ring("slab", 1), ring("slab", lax.axis_size("slab") - 1)
    below_near = lax.ppermute(high_near, "slab", up)
    above_near = lax.ppermute(low_near, "slab", down)
    own, weighted, lane, tile = pl.pallas_call(
        own_kernel,
        out_shape=[shape((9, GROUPS, T)), shape((BLOCKS, 3 * T, 256), BF16),
                   shape((BLOCKS, T, T), jnp.int16), shape((BLOCKS, T, T), jnp.int16)],
        in_specs=[VMEM] * 6, out_specs=[VMEM] * 4,
        scratch_shapes=[pltpu.VMEM((BLOCKS * STRIP, 256), BF16)]
        + [pltpu.VMEM((STRIP, BLOCKS * STRIP), BF16)] * 2 + [pltpu.VMEM((9, ATOMS, T), BF16)],
        compiler_params=PARAMS, cost_estimate=cost(12_000_000_000, 6 << 20), name="own",
    )(*halves, mode_cot.reshape(1, 256), neighbours.T)
    high_far, low_far, own = lax.optimization_barrier((high_far, low_far, own))
    below_far = lax.ppermute(high_far, "slab", up)
    above_far = lax.ppermute(low_far, "slab", down)
    slots = pair_features.shape[0]
    steps = slots // CHUNK
    rows_spec = lambda width: pl.BlockSpec((CHUNK, width), lambda s: (s, 0))
    full = lambda *dims: pl.BlockSpec(dims, lambda s: (0,) * len(dims))
    hidden, slope, turned = pl.pallas_call(
        forward_kernel, out_shape=[shape((slots, 256), BF16)] * 2 + [shape((EXT, slots), BF16)], grid=(steps,),
        in_specs=[rows_spec(128), full(128, 256), full(1, 256), anywhere],
        out_specs=[rows_spec(256)] * 2 + [pl.BlockSpec((EXT, CHUNK), lambda s: (0, s))],
        compiler_params=PARAMS, cost_estimate=cost(4_000_000_000, 8 << 20), name="forward",
    )(pair_features, w_in, b_in.reshape(1, 256), own)
    total = pl.pallas_call(
        near_kernel, out_shape=shape((9, GROUPS, T)), in_specs=[VMEM] * 6, out_specs=VMEM,
        scratch_shapes=[pltpu.VMEM((STRIP, NEAR * STRIP), BF16)] * 2 + [pltpu.VMEM((9, ATOMS, T), BF16)],
        compiler_params=PARAMS, cost_estimate=cost(4_000_000_000, 6 << 20), name="near",
    )(below_near, above_near, weighted, lane, tile, own)
    parts = pl.pallas_call(
        far_kernel, out_shape=[shape((9, QUARTER, T), BF16)] * 4,
        in_specs=[SMEM] + [VMEM] * 6 + [anywhere], out_specs=[VMEM] * 4,
        scratch_shapes=[pltpu.VMEM((STRIP, (REACH - NEAR) * STRIP), BF16)] * 2
        + [pltpu.VMEM((9, ATOMS, T), BF16), pltpu.VMEM((9, GROUPS, T), F32)],
        compiler_params=PARAMS, cost_estimate=cost(1_000_000_000, 5 << 20), name="far",
    )(m, below_far, above_far, weighted, lane, tile, total, turned)
    parts = [parts[0]] + [lax.ppermute(parts[k], "mode", ring("mode", k)) for k in (1, 2, 3)]
    pre_cot, *sums = pl.pallas_call(
        gradient_kernel,
        out_shape=[shape((slots, 256), BF16)] + [shape((ROWS, T))] * 4,
        in_specs=[SMEM] + [VMEM] * 8, out_specs=[VMEM] * 5,
        scratch_shapes=[pltpu.VMEM((QUARTER, 16, T), BF16), pltpu.VMEM((SUM_ROWS, T), F32)],
        compiler_params=PARAMS, cost_estimate=cost(2_000_000_000, 9 << 20), name="gradient",
    )(m, *parts, turned, hidden, slope, w_out)
    features_grad = pl.pallas_call(
        features_kernel, out_shape=shape((slots, 128), BF16), grid=(steps // 2,),
        in_specs=[pl.BlockSpec((2 * CHUNK, 256), lambda s: (s, 0)), full(128, 256)],
        out_specs=pl.BlockSpec((2 * CHUNK, 128), lambda s: (s, 0)),
        compiler_params=PARAMS, cost_estimate=cost(2_000_000_000, 5 << 20), name="features",
    )(pre_cot, w_in)
    share = sums[0]
    for k in (1, 2, 3):
        share = share + lax.ppermute(sums[k], "mode", ring("mode", k))
    share, features_grad = lax.optimization_barrier((share, features_grad))
    line = [[g * 8 + k for k in range(8)] for g in range(8)]
    plane = [[k * 8 + g for k in range(8)] for g in range(8)]
    for groups in (line, plane):
        spread = jnp.broadcast_to(share.astype(BF16)[None], (8, ROWS, T))
        got = lax.all_to_all(spread, "slab", 0, 0, axis_index_groups=groups, tiled=True)
        share = jnp.sum(got.astype(F32), axis=0)
    pieces = [share] + [lax.ppermute(share, "mode", ring("mode", k)) for k in (1, 2, 3)]
    grad_w_in, grad_b_in, grad_w_out = pl.pallas_call(
        finish_kernel, out_shape=[shape((128, 256)), shape((1, 256)), shape((9, 256))],
        in_specs=[SMEM] + [VMEM] * 4, out_specs=[VMEM] * 3,
        scratch_shapes=[pltpu.VMEM((SUM_ROWS, T), F32)],
        compiler_params=PARAMS, name="finish",
    )(m, *pieces)
    return (features_grad, grad_w_in, grad_b_in.reshape(256), grad_w_out)


def solution(mesh):
    return jax.shard_map(
        shards,
        mesh=mesh,
        in_specs=(
            P("slab", None, "mode"),
            P("slab"),
            P("mode"),
            P("slab", None),
            P(("slab", "mode"), None),
            P(),
            P(),
            P(),
        ),
        out_specs=(P(("slab", "mode"), None), P(), P(), P()),
        check_vma=False,
    )
```

```python
import functools

import jax
import jax.numpy as jnp
from jax import lax
from jax.experimental import pallas as pl
from jax.experimental.pallas import tpu as pltpu
from jax.sharding import PartitionSpec as P

MASS_TABLE = (1.35, 2.94, 2.79, 2.95)
CLIP_NORM = 100.0
T = 128
ATOMS = 1280
RIM = 640
BLOCKS = ATOMS // T
REACH = RIM // T
GROUPS = ATOMS // 8
QUARTER = GROUPS // 4
F32, BF16 = jnp.float32, jnp.bfloat16
VMEM = pl.BlockSpec(memory_space=pltpu.VMEM)
SMEM = pl.BlockSpec(memory_space=pltpu.SMEM)
PARAMS = pltpu.CompilerParams(vmem_limit_bytes=24 << 20)


def nt_dot(x, y):
    return lax.dot_general(x, y, (((1,), (1,)), ((), ())), preferred_element_type=F32)


def tn_dot(x, y):
    return lax.dot_general(x, y, (((0,), (0,)), ((), ())), preferred_element_type=F32)


STRIP = 3 * T


NEAR = 3


def scale_kernel(eig, species, high_near, high_far, low_near, low_far):
    order = [blk for t in range(REACH) for blk in (BLOCKS - 1 - t, t)]
    for blk in order:
        rows = slice(blk * T, (blk + 1) * T)
        kind = species[rows].reshape(1, T)
        mass = jnp.full(kind.shape, MASS_TABLE[3], F32)
        for k in range(3):
            mass = jnp.where(kind == k, MASS_TABLE[k], mass)
        inv = jnp.broadcast_to(lax.rsqrt(mass), (T, T)).T
        inv = jnp.concatenate([inv, inv], axis=1)
        out, tile = place_of(blk, high_near, high_far, low_near, low_far)
        for a in range(3):
            at = tile * STRIP + a * T
            out[at:at + T, :] = (eig[a, rows, :].astype(F32) * inv).astype(BF16)


def place_of(blk, high_near, high_far, low_near, low_far):
    if blk < NEAR:
        return low_near, blk
    if blk < REACH:
        return low_far, blk - NEAR
    if blk < BLOCKS - NEAR:
        return high_far, blk - REACH
    return high_near, blk - (BLOCKS - NEAR)


def fold_matrix():
    row = lax.broadcasted_iota(jnp.int32, (2 * T // 8, 2 * T), 0)
    col = lax.broadcasted_iota(jnp.int32, (2 * T // 8, 2 * T), 1)
    return (col // 8 == row).astype(BF16)


def pick(dense, local, a, b, at):
    place = (local * 3 + b) * T
    return dense[a * T + at:a * T + at + 16, place:place + T]


def lane_gather(values, lane):
    numbers = lax.GatherDimensionNumbers(
        offset_dims=(), collapsed_slice_dims=(1,), start_index_map=(1,),
        operand_batching_dims=(0,), start_indices_batching_dims=(0,))
    return lax.gather(values, lane[..., None], numbers, slice_sizes=(1, 1),
                      mode=lax.GatherScatterMode.PROMISE_IN_BOUNDS)


def pipeline(jobs, weighted, lane_ref, tile_ref, dense, terms, with_self):
    def multiply(job, out):
        i, rows, first, _, tiles = job
        left = weighted[i]
        for start in range(0, tiles * STRIP, 2 * STRIP):
            stop = min(start + 2 * STRIP, tiles * STRIP)
            out[:, start:stop] = nt_dot(left, rows[first + start:first + stop, :]).astype(BF16)

    def gather(job, src, at):
        i, _, _, first_tile, tiles = job
        lane, where_tile = lane_ref[i, at:at + 16, :], tile_ref[i, at:at + 16, :]
        sums = [jnp.zeros((16, T), BF16)] * 9
        for local in range(tiles):
            here = where_tile == jnp.int16(first_tile + local)
            for a in range(3):
                for b in range(3):
                    got = lane_gather(pick(src, local, a, b, at), lane)
                    sums[3 * a + b] = jnp.where(here, got, sums[3 * a + b])
        if with_self:
            mine = (lax.broadcasted_iota(jnp.int32, (16, T), 0) + at).astype(jnp.int16)
            live = where_tile.astype(jnp.int32) >= 0
            for a in range(3):
                for b in range(3):
                    got = lane_gather(pick(src, i + REACH - first_tile, a, b, at), mine)
                    term = sums[3 * a + b].astype(F32) - got.astype(F32)
                    sums[3 * a + b] = jnp.where(live, term, 0.0).astype(BF16)
        for c in range(9):
            terms[c, i * T + at:i * T + at + 16, :] = sums[c]

    multiply(jobs[0], dense[0])
    for k, job in enumerate(jobs):

        def turn(step, carry, k=k, job=job):
            if k + 1 < len(jobs):
                multiply(jobs[k + 1], dense[(k + 1) % 2])
            for at in range(0, T, 16):
                gather(job, dense[k % 2], at)
            return carry

        turn(0, 0)


def own_kernel(high_near, high_far, low_near, low_far, mode_cot, nbr_t, _after, out, weighted, lane_ref, tile_ref, stack, dense0, dense1, terms):
    row = lax.broadcasted_iota(jnp.int32, (T, T), 0)
    col = lax.broadcasted_iota(jnp.int32, (T, T), 1)
    diagonal = (row % 8) == (col // 16)
    cot = mode_cot[...]
    for blk in range(BLOCKS):
        n = nbr_t[:, blk * T:(blk + 1) * T].astype(F32)
        n = jnp.concatenate([n] * 8, axis=0).T.astype(jnp.int32)
        live = diagonal & (n < ATOMS + 2 * RIM)
        tile_ref[blk] = jnp.where(live, n >> 7, -1).astype(jnp.int16)
        lane_ref[blk] = (n & (T - 1)).astype(jnp.int16)
        src, tile = place_of(blk, high_near, high_far, low_near, low_far)
        s = src[tile * STRIP:(tile + 1) * STRIP, :]
        stack[blk * STRIP:(blk + 1) * STRIP, :] = s
        weighted[blk] = (s.astype(F32) * cot).astype(BF16)
    jobs = []
    for i in range(BLOCKS):
        first, last = max(i - REACH, 0), min(i + REACH, BLOCKS - 1)
        jobs.append((i, stack, first * STRIP, first + REACH, last - first + 1))
    pipeline(jobs, weighted, lane_ref, tile_ref, (dense0, dense1), terms, True)
    fold = fold_matrix()
    for h in range(BLOCKS // 2):
        for c in range(9):
            out[c, h * 32:(h + 1) * 32, :] = jnp.dot(
                fold, terms[c, h * 2 * T:(h + 1) * 2 * T, :], preferred_element_type=F32)


def near_kernel(below, above, weighted, lane_ref, tile_ref, own, total, dense0, dense1, terms):
    skip = REACH - NEAR
    jobs = []
    for i in reversed(range(REACH)):
        first = max(i, skip)
        jobs.append((i, below, (first - skip) * STRIP, first, REACH - first))
    for i in reversed(range(REACH, BLOCKS)):
        jobs.append((i, above, 0, 3 * REACH, min(i - REACH + 1, NEAR)))
    pipeline(jobs, weighted, lane_ref, tile_ref, (dense0, dense1), terms, False)
    fold = fold_matrix()
    for h in range(BLOCKS // 2):
        for c in range(9):
            at = slice(h * 32, (h + 1) * 32)
            total[c, at, :] = own[c, at, :] + jnp.dot(
                fold, terms[c, h * 2 * T:(h + 1) * 2 * T, :], preferred_element_type=F32)


def far_kernel(mode_index, below, above, weighted, lane_ref, tile_ref, before,
               out0, out1, out2, out3, dense0, dense1, terms, total):
    skip = REACH - NEAR
    jobs = [(i, below, i * STRIP, i, skip - i) for i in reversed(range(skip))]
    jobs += [(i, above, 0, 3 * REACH + NEAR, i - REACH - NEAR + 1) for i in range(REACH + NEAR, BLOCKS)]
    pipeline(jobs, weighted, lane_ref, tile_ref, (dense0, dense1), terms, False)
    total[...] = before[...]
    fold = fold_matrix()
    for h in (0, BLOCKS // 2 - 1):
        for c in range(9):
            at = slice(h * 32, (h + 1) * 32)
            total[c, at, :] += jnp.dot(
                fold, terms[c, h * 2 * T:(h + 1) * 2 * T, :], preferred_element_type=F32)
    m = mode_index[0]
    for k, out in enumerate((out0, out1, out2, out3)):
        q = lax.rem(m + k, 4)
        out[...] = total[:, pl.ds(pl.multiple_of(q * QUARTER, 8), QUARTER), :].astype(BF16)


CHUNK = 512
EXT = 144


def forward_kernel(features, w_in, b_in, hidden, slope, turned):
    x = features[...]
    pre = jnp.dot(x, w_in[...], preferred_element_type=F32) + b_in[...]
    sig = 1.0 / (1.0 + jnp.exp(-pre))
    hidden[...] = (pre * sig).astype(BF16)
    slope[...] = (sig * (1.0 + pre * (1.0 - sig))).astype(BF16)
    turned[0:128, :] = x.T
    row = lax.broadcasted_iota(jnp.int32, (EXT - 128, CHUNK), 0)
    turned[128:EXT, :] = (row == 0).astype(BF16)


def gradient_kernel(mode_index, p0, p1, p2, p3, turned, hidden, slope, w_out,
                    pre_cot, g0, g1, g2, g3, cot, sums):
    whole = sum(p[...].astype(F32) for p in (p0, p1, p2, p3))
    whole = jnp.concatenate([whole, jnp.zeros((7, QUARTER, T), F32)], axis=0)
    cot[...] = jnp.swapaxes(whole, 0, 1).astype(BF16)
    sums[...] = jnp.zeros_like(sums)
    w_out16 = jnp.concatenate([w_out[...].astype(F32), jnp.zeros((7, 256), F32)], axis=0).astype(BF16)
    per = CHUNK // T
    total_in, total_out = jnp.zeros((EXT, 256), F32), jnp.zeros((16, 256), F32)
    for step in range(hidden.shape[0] // CHUNK):
        rows = slice(step * CHUNK, (step + 1) * CHUNK)
        pair_cot = jnp.concatenate([cot[step * per + g] for g in range(per)], axis=1)
        part = (tn_dot(pair_cot, w_out16) * slope[rows, :].astype(F32)).astype(BF16)
        pre_cot[rows, :] = part
        total_in += jnp.dot(turned[:, rows], part, preferred_element_type=F32)
        total_out += jnp.dot(pair_cot, hidden[rows, :], preferred_element_type=F32)
    for h in range(2):
        cols = slice(h * T, (h + 1) * T)
        sums[h * 152:h * 152 + 128, :] = total_in[0:128, cols]
        sums[h * 152 + 128:h * 152 + 144, :] = total_out[:, cols]
        sums[h * 152 + 144:h * 152 + 152, :] = total_in[128:136, cols]
    m = mode_index[0]
    for k, out in enumerate((g0, g1, g2, g3)):
        q = lax.rem(m + k, 4)
        out[...] = sums[pl.ds(pl.multiple_of(q * ROWS, 8), ROWS), :]


def features_kernel(pre_cot, w_in, grad):
    grad[...] = nt_dot(pre_cot[...], w_in[...]).astype(BF16)


SUM_ROWS = 320
ROWS = SUM_ROWS // 4


def finish_kernel(mode_index, c0, c1, c2, c3, grad_w_in, grad_b_in, grad_w_out, whole):
    m = mode_index[0]
    for k, part in enumerate((c0, c1, c2, c3)):
        q = lax.rem(m + 4 - k, 4)
        whole[pl.ds(pl.multiple_of(q * ROWS, 8), ROWS), :] = part[...]
    both = []
    for start, rows in ((0, 128), (128, 9), (144, 1)):
        both.append(jnp.concatenate([whole[h * 152 + start:h * 152 + start + rows, :] for h in range(2)], axis=1))
    w, o, b = both
    norm_sq = jnp.sum(w * w) + jnp.sum(b * b) + jnp.sum(o * o)
    factor = jnp.minimum(1.0, CLIP_NORM / jnp.sqrt(jnp.broadcast_to(norm_sq + 1e-06, (1, 256))))
    grad_w_in[...] = w * factor
    grad_b_in[...] = b * factor
    grad_w_out[...] = o * factor


def shape(dims, dtype=F32):
    return jax.ShapeDtypeStruct(dims, dtype)


def cost(flops, moved):
    return pl.CostEstimate(flops=flops, bytes_accessed=moved, transcendentals=0)


def ring(axis, k):
    n = lax.axis_size(axis)
    return [(i, (i + k) % n) for i in range(n)]


def shards(eigvec, species, mode_cot, neighbours, pair_features, w_in, b_in, w_out):
    eig = jnp.transpose(eigvec, (1, 0, 2))
    m = lax.axis_index("mode").astype(jnp.int32).reshape(1)
    near, far = NEAR * STRIP, (REACH - NEAR) * STRIP
    anywhere = pl.BlockSpec(memory_space=pl.ANY)
    halves = pl.pallas_call(
        scale_kernel, out_shape=[shape((near, 256), BF16), shape((far, 256), BF16)] * 2,
        in_specs=[VMEM] * 2, out_specs=[VMEM] * 4,
        compiler_params=PARAMS, cost_estimate=cost(1 << 20, 4 << 20), name="scale",
    )(eig, species)
    high_near, high_far, low_near, low_far = halves
    up, down = ring("slab", 1), ring("slab", lax.axis_size("slab") - 1)
    below_near = lax.ppermute(high_near, "slab", up)
    above_near = lax.ppermute(low_near, "slab", down)
    slots = pair_features.shape[0]
    steps = slots // CHUNK
    rows_spec = lambda width: pl.BlockSpec((CHUNK, width), lambda s: (s, 0))
    full = lambda *dims: pl.BlockSpec(dims, lambda s: (0,) * len(dims))
    hidden, slope, turned = pl.pallas_call(
        forward_kernel, out_shape=[shape((slots, 256), BF16)] * 2 + [shape((EXT, slots), BF16)], grid=(steps,),
        in_specs=[rows_spec(128), full(128, 256), full(1, 256)],
        out_specs=[rows_spec(256)] * 2 + [pl.BlockSpec((EXT, CHUNK), lambda s: (0, s))],
        compiler_params=PARAMS, cost_estimate=cost(4_000_000_000, 8 << 20), name="forward",
    )(pair_features, w_in, b_in.reshape(1, 256))
    high_far, low_far, turned = lax.optimization_barrier((high_far, low_far, turned))
    below_far = lax.ppermute(high_far, "slab", up)
    above_far = lax.ppermute(low_far, "slab", down)
    own, weighted, lane, tile = pl.pallas_call(
        own_kernel,
        out_shape=[shape((9, GROUPS, T)), shape((BLOCKS, 3 * T, 256), BF16),
                   shape((BLOCKS, T, T), jnp.int16), shape((BLOCKS, T, T), jnp.int16)],
        in_specs=[VMEM] * 6 + [anywhere], out_specs=[VMEM] * 4,
        scratch_shapes=[pltpu.VMEM((BLOCKS * STRIP, 256), BF16)]
        + [pltpu.VMEM((STRIP, BLOCKS * STRIP), BF16)] * 2 + [pltpu.VMEM((9, ATOMS, T), BF16)],
        compiler_params=PARAMS, cost_estimate=cost(12_000_000_000, 6 << 20), name="own",
    )(high_near, high_far, low_near, low_far, mode_cot.reshape(1, 256), neighbours.T, turned)
    total = pl.pallas_call(
        near_kernel, out_shape=shape((9, GROUPS, T)), in_specs=[VMEM] * 6, out_specs=VMEM,
        scratch_shapes=[pltpu.VMEM((STRIP, NEAR * STRIP), BF16)] * 2 + [pltpu.VMEM((9, ATOMS, T), BF16)],
        compiler_params=PARAMS, cost_estimate=cost(4_000_000_000, 6 << 20), name="near",
    )(below_near, above_near, weighted, lane, tile, own)
    parts = pl.pallas_call(
        far_kernel, out_shape=[shape((9, QUARTER, T), BF16)] * 4,
        in_specs=[SMEM] + [VMEM] * 6, out_specs=[VMEM] * 4,
        scratch_shapes=[pltpu.VMEM((STRIP, (REACH - NEAR) * STRIP), BF16)] * 2
        + [pltpu.VMEM((9, ATOMS, T), BF16), pltpu.VMEM((9, GROUPS, T), F32)],
        compiler_params=PARAMS, cost_estimate=cost(1_000_000_000, 5 << 20), name="far",
    )(m, below_far, above_far, weighted, lane, tile, total)
    parts = [parts[0]] + [lax.ppermute(parts[k], "mode", ring("mode", k)) for k in (1, 2, 3)]
    pre_cot, *sums = pl.pallas_call(
        gradient_kernel,
        out_shape=[shape((slots, 256), BF16)] + [shape((ROWS, T))] * 4,
        in_specs=[SMEM] + [VMEM] * 8, out_specs=[VMEM] * 5,
        scratch_shapes=[pltpu.VMEM((QUARTER, 16, T), BF16), pltpu.VMEM((SUM_ROWS, T), F32)],
        compiler_params=PARAMS, cost_estimate=cost(2_000_000_000, 9 << 20), name="gradient",
    )(m, *parts, turned, hidden, slope, w_out)
    features_grad = pl.pallas_call(
        features_kernel, out_shape=shape((slots, 128), BF16), grid=(steps // 2,),
        in_specs=[pl.BlockSpec((2 * CHUNK, 256), lambda s: (s, 0)), full(128, 256)],
        out_specs=pl.BlockSpec((2 * CHUNK, 128), lambda s: (s, 0)),
        compiler_params=PARAMS, cost_estimate=cost(2_000_000_000, 5 << 20), name="features",
    )(pre_cot, w_in)
    share = sums[0]
    for k in (1, 2, 3):
        share = share + lax.ppermute(sums[k], "mode", ring("mode", k))
    line = [[g * 8 + k for k in range(8)] for g in range(8)]
    plane = [[k * 8 + g for k in range(8)] for g in range(8)]
    for groups in (line, plane):
        spread = jnp.broadcast_to(share.astype(BF16)[None], (8, ROWS, T))
        got = lax.all_to_all(spread, "slab", 0, 0, axis_index_groups=groups, tiled=True)
        share = jnp.sum(got.astype(F32), axis=0)
    pieces = [share] + [lax.ppermute(share, "mode", ring("mode", k)) for k in (1, 2, 3)]
    grad_w_in, grad_b_in, grad_w_out = pl.pallas_call(
        finish_kernel, out_shape=[shape((128, 256)), shape((1, 256)), shape((9, 256))],
        in_specs=[SMEM] + [VMEM] * 4, out_specs=[VMEM] * 3,
        scratch_shapes=[pltpu.VMEM((SUM_ROWS, T), F32)],
        compiler_params=PARAMS, name="finish",
    )(m, *pieces)
    return (features_grad, grad_w_in, grad_b_in.reshape(256), grad_w_out)


def solution(mesh):
    return jax.shard_map(
        shards,
        mesh=mesh,
        in_specs=(
            P("slab", None, "mode"),
            P("slab"),
            P("mode"),
            P("slab", None),
            P(("slab", "mode"), None),
            P(),
            P(),
            P(),
        ),
        out_specs=(P(("slab", "mode"), None), P(), P(), P()),
        check_vma=False,
    )
```

```python
import functools

import jax
import jax.numpy as jnp
from jax import lax
from jax.experimental import pallas as pl
from jax.experimental.pallas import tpu as pltpu
from jax.sharding import PartitionSpec as P

MASS_TABLE = (1.35, 2.94, 2.79, 2.95)
CLIP_NORM = 100.0
T = 128
ATOMS = 1280
RIM = 640
BLOCKS = ATOMS // T
REACH = RIM // T
GROUPS = ATOMS // 8
QUARTER = GROUPS // 4
F32, BF16 = jnp.float32, jnp.bfloat16
VMEM = pl.BlockSpec(memory_space=pltpu.VMEM)
SMEM = pl.BlockSpec(memory_space=pltpu.SMEM)
PARAMS = pltpu.CompilerParams(vmem_limit_bytes=24 << 20)


def nt_dot(x, y):
    return lax.dot_general(x, y, (((1,), (1,)), ((), ())), preferred_element_type=F32)


def tn_dot(x, y):
    return lax.dot_general(x, y, (((0,), (0,)), ((), ())), preferred_element_type=F32)


STRIP = 3 * T


def scale_kernel(eig, species, high, low):
    def half(base, out):
        for blk in range(REACH):
            rows = slice(base + blk * T, base + (blk + 1) * T)
            kind = species[rows].reshape(1, T)
            mass = jnp.full(kind.shape, MASS_TABLE[3], F32)
            for k in range(3):
                mass = jnp.where(kind == k, MASS_TABLE[k], mass)
            inv = jnp.broadcast_to(lax.rsqrt(mass), (T, T)).T
            inv = jnp.concatenate([inv, inv], axis=1)
            for a in range(3):
                at = blk * STRIP + a * T
                out[at:at + T, :] = (eig[a, rows, :].astype(F32) * inv).astype(BF16)

    half(RIM, high)
    half(0, low)


def fold_matrix():
    row = lax.broadcasted_iota(jnp.int32, (2 * T // 8, 2 * T), 0)
    col = lax.broadcasted_iota(jnp.int32, (2 * T // 8, 2 * T), 1)
    return (col // 8 == row).astype(BF16)


def pick(dense, local, a, b, at):
    place = (local * 3 + b) * T
    return dense[a * T + at:a * T + at + 16, place:place + T]


def lane_gather(values, lane):
    numbers = lax.GatherDimensionNumbers(
        offset_dims=(), collapsed_slice_dims=(1,), start_index_map=(1,),
        operand_batching_dims=(0,), start_indices_batching_dims=(0,))
    return lax.gather(values, lane[..., None], numbers, slice_sizes=(1, 1),
                      mode=lax.GatherScatterMode.PROMISE_IN_BOUNDS)


def pipeline(jobs, weighted, lane_ref, tile_ref, dense, terms, with_self):
    def multiply(job, out):
        i, rows, first, _, tiles = job
        left = weighted[i]
        for start in range(0, tiles * STRIP, 2 * STRIP):
            stop = min(start + 2 * STRIP, tiles * STRIP)
            out[:, start:stop] = nt_dot(left, rows[first + start:first + stop, :]).astype(BF16)

    def gather(job, src, at):
        i, _, _, first_tile, tiles = job
        lane, where_tile = lane_ref[i, at:at + 16, :], tile_ref[i, at:at + 16, :]
        sums = [jnp.zeros((16, T), BF16)] * 9
        for local in range(tiles):
            here = where_tile == jnp.int16(first_tile + local)
            for a in range(3):
                for b in range(3):
                    got = lane_gather(pick(src, local, a, b, at), lane)
                    sums[3 * a + b] = jnp.where(here, got, sums[3 * a + b])
        if with_self:
            mine = (lax.broadcasted_iota(jnp.int32, (16, T), 0) + at).astype(jnp.int16)
            live = where_tile.astype(jnp.int32) >= 0
            for a in range(3):
                for b in range(3):
                    got = lane_gather(pick(src, i + REACH - first_tile, a, b, at), mine)
                    term = sums[3 * a + b].astype(F32) - got.astype(F32)
                    sums[3 * a + b] = jnp.where(live, term, 0.0).astype(BF16)
        for c in range(9):
            terms[c, i * T + at:i * T + at + 16, :] = sums[c]

    multiply(jobs[0], dense[0])
    for k, job in enumerate(jobs):

        def turn(step, carry, k=k, job=job):
            if k + 1 < len(jobs):
                multiply(jobs[k + 1], dense[(k + 1) % 2])
            for at in range(0, T, 16):
                gather(job, dense[k % 2], at)
            return carry

        turn(0, 0)


def own_kernel(high, low, mode_cot, nbr_t, out, weighted, lane_ref, tile_ref, stack, dense0, dense1, terms):
    row = lax.broadcasted_iota(jnp.int32, (T, T), 0)
    col = lax.broadcasted_iota(jnp.int32, (T, T), 1)
    diagonal = (row % 8) == (col // 16)
    cot = mode_cot[...]
    for blk in range(BLOCKS):
        n = nbr_t[:, blk * T:(blk + 1) * T].astype(F32)
        n = jnp.concatenate([n] * 8, axis=0).T.astype(jnp.int32)
        live = diagonal & (n < ATOMS + 2 * RIM)
        tile_ref[blk] = jnp.where(live, n >> 7, -1).astype(jnp.int16)
        lane_ref[blk] = (n & (T - 1)).astype(jnp.int16)
        src = low if blk < REACH else high
        s = src[blk % REACH * STRIP:(blk % REACH + 1) * STRIP, :]
        stack[blk * STRIP:(blk + 1) * STRIP, :] = s
        weighted[blk] = (s.astype(F32) * cot).astype(BF16)
    jobs = []
    for i in range(BLOCKS):
        first, last = max(i - REACH, 0), min(i + REACH, BLOCKS - 1)
        jobs.append((i, stack, first * STRIP, first + REACH, last - first + 1))
    pipeline(jobs, weighted, lane_ref, tile_ref, (dense0, dense1), terms, True)
    fold = fold_matrix()
    for h in range(BLOCKS // 2):
        for c in range(9):
            out[c, h * 32:(h + 1) * 32, :] = jnp.dot(
                fold, terms[c, h * 2 * T:(h + 1) * 2 * T, :], preferred_element_type=F32)


def halo_kernel(mode_index, below, above, weighted, lane_ref, tile_ref, own, _after,
                out0, out1, out2, out3, dense0, dense1, terms, total):
    jobs = [(i, below, i * STRIP, i, REACH - i) for i in reversed(range(REACH))]
    jobs += [(i, above, 0, 3 * REACH, i - REACH + 1) for i in reversed(range(REACH, BLOCKS))]
    pipeline(jobs, weighted, lane_ref, tile_ref, (dense0, dense1), terms, False)
    fold = fold_matrix()
    for h in range(BLOCKS // 2):
        for c in range(9):
            at = slice(h * 32, (h + 1) * 32)
            total[c, at, :] = own[c, at, :] + jnp.dot(
                fold, terms[c, h * 2 * T:(h + 1) * 2 * T, :], preferred_element_type=F32)
    m = mode_index[0]
    for k, out in enumerate((out0, out1, out2, out3)):
        q = lax.rem(m + k, 4)
        out[...] = total[:, pl.ds(pl.multiple_of(q * QUARTER, 8), QUARTER), :].astype(BF16)


CHUNK = 512
EXT = 144


def forward_kernel(features, w_in, b_in, hidden, slope, turned):
    x = features[...]
    pre = jnp.dot(x, w_in[...], preferred_element_type=F32) + b_in[...]
    sig = 1.0 / (1.0 + jnp.exp(-pre))
    hidden[...] = (pre * sig).astype(BF16)
    slope[...] = (sig * (1.0 + pre * (1.0 - sig))).astype(BF16)
    turned[0:128, :] = x.T
    row = lax.broadcasted_iota(jnp.int32, (EXT - 128, CHUNK), 0)
    turned[128:EXT, :] = (row == 0).astype(BF16)


def gradient_kernel(mode_index, p0, p1, p2, p3, turned, hidden, slope, w_out,
                    pre_cot, g0, g1, g2, g3, cot, sums):
    whole = sum(p[...].astype(F32) for p in (p0, p1, p2, p3))
    whole = jnp.concatenate([whole, jnp.zeros((7, QUARTER, T), F32)], axis=0)
    cot[...] = jnp.swapaxes(whole, 0, 1).astype(BF16)
    sums[...] = jnp.zeros_like(sums)
    w_out16 = jnp.concatenate([w_out[...].astype(F32), jnp.zeros((7, 256), F32)], axis=0).astype(BF16)
    per = CHUNK // T
    total_in, total_out = jnp.zeros((EXT, 256), F32), jnp.zeros((16, 256), F32)
    for step in range(hidden.shape[0] // CHUNK):
        rows = slice(step * CHUNK, (step + 1) * CHUNK)
        pair_cot = jnp.concatenate([cot[step * per + g] for g in range(per)], axis=1)
        part = (tn_dot(pair_cot, w_out16) * slope[rows, :].astype(F32)).astype(BF16)
        pre_cot[rows, :] = part
        total_in += jnp.dot(turned[:, rows], part, preferred_element_type=F32)
        total_out += jnp.dot(pair_cot, hidden[rows, :], preferred_element_type=F32)
    for h in range(2):
        cols = slice(h * T, (h + 1) * T)
        sums[h * 152:h * 152 + 128, :] = total_in[0:128, cols]
        sums[h * 152 + 128:h * 152 + 144, :] = total_out[:, cols]
        sums[h * 152 + 144:h * 152 + 152, :] = total_in[128:136, cols]
    m = mode_index[0]
    for k, out in enumerate((g0, g1, g2, g3)):
        q = lax.rem(m + k, 4)
        out[...] = sums[pl.ds(pl.multiple_of(q * ROWS, 8), ROWS), :]


def features_kernel(pre_cot, w_in, grad):
    grad[...] = nt_dot(pre_cot[...], w_in[...]).astype(BF16)


SUM_ROWS = 320
ROWS = SUM_ROWS // 4


def finish_kernel(mode_index, c0, c1, c2, c3, grad_w_in, grad_b_in, grad_w_out, whole):
    m = mode_index[0]
    for k, part in enumerate((c0, c1, c2, c3)):
        q = lax.rem(m + 4 - k, 4)
        whole[pl.ds(pl.multiple_of(q * ROWS, 8), ROWS), :] = part[...]
    both = []
    for start, rows in ((0, 128), (128, 9), (144, 1)):
        both.append(jnp.concatenate([whole[h * 152 + start:h * 152 + start + rows, :] for h in range(2)], axis=1))
    w, o, b = both
    norm_sq = jnp.sum(w * w) + jnp.sum(b * b) + jnp.sum(o * o)
    factor = jnp.minimum(1.0, CLIP_NORM / jnp.sqrt(jnp.broadcast_to(norm_sq + 1e-06, (1, 256))))
    grad_w_in[...] = w * factor
    grad_b_in[...] = b * factor
    grad_w_out[...] = o * factor


def shape(dims, dtype=F32):
    return jax.ShapeDtypeStruct(dims, dtype)


def cost(flops, moved):
    return pl.CostEstimate(flops=flops, bytes_accessed=moved, transcendentals=0)


def ring(axis, k):
    n = lax.axis_size(axis)
    return [(i, (i + k) % n) for i in range(n)]


def shards(eigvec, species, mode_cot, neighbours, pair_features, w_in, b_in, w_out):
    eig = jnp.transpose(eigvec, (1, 0, 2))
    m = lax.axis_index("mode").astype(jnp.int32).reshape(1)
    high, low = pl.pallas_call(
        scale_kernel, out_shape=[shape((REACH * STRIP, 256), BF16)] * 2,
        in_specs=[VMEM] * 2, out_specs=[VMEM] * 2, compiler_params=PARAMS,
        cost_estimate=cost(1 << 20, 4 << 20), name="scale",
    )(eig, species)
    below = lax.ppermute(high, "slab", ring("slab", 1))
    above = lax.ppermute(low, "slab", ring("slab", lax.axis_size("slab") - 1))
    own, weighted, lane, tile = pl.pallas_call(
        own_kernel,
        out_shape=[shape((9, GROUPS, T)), shape((BLOCKS, 3 * T, 256), BF16),
                   shape((BLOCKS, T, T), jnp.int16), shape((BLOCKS, T, T), jnp.int16)],
        in_specs=[VMEM] * 4, out_specs=[VMEM] * 4,
        scratch_shapes=[pltpu.VMEM((BLOCKS * STRIP, 256), BF16)]
        + [pltpu.VMEM((STRIP, BLOCKS * STRIP), BF16)] * 2 + [pltpu.VMEM((9, ATOMS, T), BF16)],
        compiler_params=PARAMS, cost_estimate=cost(12_000_000_000, 6 << 20), name="own",
    )(high, low, mode_cot.reshape(1, 256), neighbours.T)
    slots = pair_features.shape[0]
    steps = slots // CHUNK
    rows_spec = lambda width: pl.BlockSpec((CHUNK, width), lambda s: (s, 0))
    full = lambda *dims: pl.BlockSpec(dims, lambda s: (0,) * len(dims))
    hidden, slope, turned = pl.pallas_call(
        forward_kernel, out_shape=[shape((slots, 256), BF16)] * 2 + [shape((EXT, slots), BF16)], grid=(steps,),
        in_specs=[rows_spec(128), full(128, 256), full(1, 256)],
        out_specs=[rows_spec(256)] * 2 + [pl.BlockSpec((EXT, CHUNK), lambda s: (0, s))],
        compiler_params=PARAMS, cost_estimate=cost(4_000_000_000, 8 << 20), name="forward",
    )(pair_features, w_in, b_in.reshape(1, 256))
    parts = pl.pallas_call(
        halo_kernel, out_shape=[shape((9, QUARTER, T), BF16)] * 4,
        in_specs=[SMEM] + [VMEM] * 6 + [pl.BlockSpec(memory_space=pl.ANY)], out_specs=[VMEM] * 4,
        scratch_shapes=[pltpu.VMEM((STRIP, REACH * STRIP), BF16)] * 2
        + [pltpu.VMEM((9, ATOMS, T), BF16), pltpu.VMEM((9, GROUPS, T), F32)],
        compiler_params=PARAMS, cost_estimate=cost(5_000_000_000, 6 << 20), name="halo",
    )(m, below, above, weighted, lane, tile, own, turned)
    parts = [parts[0]] + [lax.ppermute(parts[k], "mode", ring("mode", k)) for k in (1, 2, 3)]
    pre_cot, *sums = pl.pallas_call(
        gradient_kernel,
        out_shape=[shape((slots, 256), BF16)] + [shape((ROWS, T))] * 4,
        in_specs=[SMEM] + [VMEM] * 8, out_specs=[VMEM] * 5,
        scratch_shapes=[pltpu.VMEM((QUARTER, 16, T), BF16), pltpu.VMEM((SUM_ROWS, T), F32)],
        compiler_params=PARAMS, cost_estimate=cost(2_000_000_000, 9 << 20), name="gradient",
    )(m, *parts, turned, hidden, slope, w_out)
    features_grad = pl.pallas_call(
        features_kernel, out_shape=shape((slots, 128), BF16), grid=(steps // 2,),
        in_specs=[pl.BlockSpec((2 * CHUNK, 256), lambda s: (s, 0)), full(128, 256)],
        out_specs=pl.BlockSpec((2 * CHUNK, 128), lambda s: (s, 0)),
        compiler_params=PARAMS, cost_estimate=cost(2_000_000_000, 5 << 20), name="features",
    )(pre_cot, w_in)
    share = sums[0]
    for k in (1, 2, 3):
        share = share + lax.ppermute(sums[k], "mode", ring("mode", k))
    line = [[g * 8 + k for k in range(8)] for g in range(8)]
    plane = [[k * 8 + g for k in range(8)] for g in range(8)]
    for groups in (line, plane):
        spread = jnp.broadcast_to(share.astype(BF16)[None], (8, ROWS, T))
        got = lax.all_to_all(spread, "slab", 0, 0, axis_index_groups=groups, tiled=True)
        share = jnp.sum(got.astype(F32), axis=0)
    pieces = [share] + [lax.ppermute(share, "mode", ring("mode", k)) for k in (1, 2, 3)]
    grad_w_in, grad_b_in, grad_w_out = pl.pallas_call(
        finish_kernel, out_shape=[shape((128, 256)), shape((1, 256)), shape((9, 256))],
        in_specs=[SMEM] + [VMEM] * 4, out_specs=[VMEM] * 3,
        scratch_shapes=[pltpu.VMEM((SUM_ROWS, T), F32)],
        compiler_params=PARAMS, name="finish",
    )(m, *pieces)
    return (features_grad, grad_w_in, grad_b_in.reshape(256), grad_w_out)


def solution(mesh):
    return jax.shard_map(
        shards,
        mesh=mesh,
        in_specs=(
            P("slab", None, "mode"),
            P("slab"),
            P("mode"),
            P("slab", None),
            P(("slab", "mode"), None),
            P(),
            P(),
            P(),
        ),
        out_specs=(P(("slab", "mode"), None), P(), P(), P()),
        check_vma=False,
    )
```
